32 devices in a mesh: grp: 2 (over y), lon: 4 (over x, core), lat: 4 (over z).
Axes of the slice: x: 2, y: 2, z: 4, core: 2. Of those that a mesh axis runs over, the one named last changes fastest.
Arguments:
- state: float32 [128, 720, 256], P(('grp', 'lat'), 'lon'), parts along dimension 0, may hold values from -6 to 6
- norm_gain: float32 [1, 2, 256], replicated, may hold values from 0.25 to 1.75
- disco_kernel: float32 [1, 64, 24, 8], P(None, 'lat'), may hold values from -1.25 to 1.25
- taps: int32 [64, 24], P('lat'), may hold values from 0 to 50
- counts: int32 [64], P('lat'), may hold values from 6 to 24, as said below
- disco_mix: bfloat16 [1, 2048, 256], replicated, may hold values from -0.125 to 0.125
- filter_gain: float32 [1, 256, 256], replicated, may hold values from -0.9 to 0.9
- mlp_in: bfloat16 [1, 256, 512], replicated, may hold values from -0.375 to 0.375
- mlp_out: bfloat16 [1, 512, 256], replicated, may hold values from -0.25 to 0.25
Outputs:
- new_state: float32 [128, 720, 256], P(('grp', 'lat'), 'lon'), parts along dimension 0
The draws below stay inside these ranges and needn't reach their ends.
There are 2 independent parts, one for each index of `grp`. The reference program is written for one: setup_inputs(seed, part) draws one part's arguments, and reference() takes and returns one part's arrays. A program takes and returns all parts, laid end to end along the dimension named above; an argument that names none is the same for every part. Nothing has to cross between parts.
Inputs may be any that keep to these rules, and one draw needn't show every extreme that they name: `taps`: slot s of row i names a tap as (a + 1) * 17 + d + 8, row offset a in -1..1 and longitude offset d in -8..8; only the first counts[i] slots of a row are live. The first and last rows of the grid have 24 live slots; counts grow toward those rows.
All inputs are finite; a program needn't handle non-finite values.
Results may differ from the reference program's by a relative error of at most 0.0042.
Values may be sent and summed in bfloat16 or wider, within the bound.
A program may use at most 384 MiB of HBM per device.

```python
import math
import jax
import jax.numpy as jnp
from jax import lax

C = 256
NLON = 720
M = 256
L = 256
K = 8
HID = 512
R = 8
S = 24
BLOCKS = 1
NLAT = 64
NTAP = 51
SLABS = 4


def draw_counts(key, part):
    key = jax.random.fold_in(key, 11)
    row_ids = jnp.arange(NLAT, dtype=jnp.int32)
    distance = jnp.abs(2 * row_ids - (NLAT - 1))
    base_count = S // 4 + (S - S // 4) * distance // max(NLAT - 1, 1)
    jitter = jax.random.randint(key, (NLAT,), 0, 3, dtype=jnp.int32)
    lowered = jnp.where(base_count < S, base_count - jitter, base_count)
    return jnp.maximum(lowered, S // 4).astype(jnp.int32)


def with_ends(drawn, key, least, largest):
    spot = [jax.random.randint(jax.random.fold_in(key, axis), (), 0, length) for axis, length in enumerate(drawn.shape)]
    longest = drawn.shape.index(max(drawn.shape))
    neighbour = spot[:longest] + [(spot[longest] + 1) % drawn.shape[longest]] + spot[longest + 1:]
    return drawn.at[tuple(spot)].set(least).at[tuple(neighbour)].set(largest)


def levels(stream_key, shape, shards, smallest, high):
    factor_of, own = 1.0, jax.random.fold_in(stream_key, 6)
    for dim, shards_of in shards:
        draws = jnp.exp(jax.random.uniform(jax.random.fold_in(own, dim), (shards_of,), jnp.float32, smallest / len(shards), high / len(shards)))
        factor_of = factor_of * jnp.repeat(draws, shape[dim] // shards_of).reshape([-1 if axis == dim else 1 for axis in range(len(shape))])
    return factor_of


def gaussian(rng, dims, width, limit, cuts=(), kind=jnp.bfloat16):
    result = width * jax.random.normal(rng, dims, jnp.float32)
    if cuts:
        result = result * levels(rng, dims, cuts, -0.22, 0.18)
    return jnp.clip(result, -limit, limit).astype(kind)


def setup_inputs(seed: int = 0, part: int = 0) -> dict:
    arg_keys = jax.random.split(jax.random.key(seed), 10)
    part_keys = jax.random.split(jax.random.fold_in(arg_keys[9], part), 10)
    state = gaussian(part_keys[0], (NLAT, NLON, C), 1.0, 6.0, ((0, 4), (1, 4)), jnp.float32)
    norm_gain = jnp.clip(1.0 + 0.15 * jax.random.normal(arg_keys[1], (BLOCKS, 2, C), jnp.float32), 0.25, 1.75)
    disco_kernel = gaussian(arg_keys[2], (BLOCKS, NLAT, S, K), S ** -0.5, 1.25, ((1, 4),), jnp.float32)
    taps = with_ends(jax.random.randint(arg_keys[3], (NLAT, S), 0, NTAP), jax.random.fold_in(arg_keys[3], 1), 0, NTAP - 1).astype(jnp.int32)
    counts = draw_counts(jax.random.fold_in(arg_keys[9], 71), part)
    disco_mix = gaussian(arg_keys[5], (BLOCKS, K * C, C), (K * C) ** -0.5, 0.125)
    filter_gain = gaussian(arg_keys[6], (BLOCKS, L, C), 0.15, 0.9, (), jnp.float32)
    mlp_in = gaussian(arg_keys[7], (BLOCKS, C, HID), C ** -0.5, 0.375)
    mlp_out = gaussian(arg_keys[8], (BLOCKS, HID, C), HID ** -0.5, 0.25)
    return {"state": state, "norm_gain": norm_gain, "disco_kernel": disco_kernel, "taps": taps, "counts": counts, "disco_mix": disco_mix, "filter_gain": filter_gain, "mlp_in": mlp_in, "mlp_out": mlp_out}


exact_prec = lax.Precision.HIGHEST

def layer_norm(values, gain):
    center = values - lax.optimization_barrier(jnp.mean(values, axis=-1, keepdims=True))
    spread = lax.optimization_barrier(jnp.mean(center * center, axis=-1, keepdims=True))
    return center * lax.rsqrt(spread + 1e-05) * gain

def trig_table(mode_ids, lon_points, lon_total):
    product = mode_ids[:, None] * lon_points[None, :] % lon_total
    angles = product.astype(jnp.float32) * (2.0 * math.pi / lon_total)
    return (jnp.cos(angles), jnp.sin(angles))

def quad_weights(lat_count):
    row_ids = jnp.arange(lat_count).astype(jnp.float32)
    colatitude = math.pi * (row_ids + 0.5) / lat_count
    return math.pi * jnp.sin(colatitude) / lat_count

def legendre_table(mode_ids, lat_count, degrees):
    row_ids = jnp.arange(lat_count).astype(jnp.float32)
    colatitude = math.pi * (row_ids + 0.5) / lat_count
    cosine = jnp.cos(colatitude)[None, :]
    sine_val = jnp.sin(colatitude)[None, :]
    orders = mode_ids.astype(jnp.float32)[:, None]
    factor_ids = jnp.arange(1, degrees + 1).astype(jnp.float32)[None, :]
    log_terms = jnp.where(factor_ids <= orders, 0.5 * jnp.log((2.0 * factor_ids - 1.0) / (2.0 * factor_ids)), 0.0)
    log_start = 0.5 * jnp.log((2.0 * orders + 1.0) / (4.0 * math.pi)) + lax.optimization_barrier(jnp.sum(log_terms, axis=1, keepdims=True))
    diagonal = jnp.exp(log_start + orders * jnp.log(sine_val))

    def advance(carry, degree):
        latest, earlier = carry
        deg_sq = degree * degree
        ord_sq = orders * orders
        upper_coef = jnp.sqrt((4.0 * deg_sq - 1.0) / jnp.maximum(deg_sq - ord_sq, 1.0))
        previous = degree - 1.0
        lower_coef = jnp.sqrt(jnp.maximum(previous * previous - ord_sq, 0.0) / jnp.maximum(4.0 * previous * previous - 1.0, 1.0))
        recurred = upper_coef * (cosine * latest - lower_coef * earlier)
        second_row = cosine * jnp.sqrt(2.0 * orders + 3.0) * latest
        current = jnp.where(degree < orders, 0.0, jnp.where(degree == orders, diagonal, jnp.where(degree == orders + 1.0, second_row, recurred)))
        return ((current, latest), current)
    blank_rows = jnp.zeros_like(diagonal)
    closing, values = lax.scan(advance, (blank_rows, blank_rows), jnp.arange(degrees).astype(jnp.float32))
    return jnp.transpose(values, (1, 0, 2))

def reference(state, norm_gain, disco_kernel, taps, counts, disco_mix, filter_gain, mlp_in, mlp_out):
    tap_span = 2 * R + 1
    tap_count = 3 * tap_span
    slab_width = NLON // SLABS
    live_slots = jnp.arange(S, dtype=jnp.int32)[None, :] < counts[:, None]
    matches = (taps[:, :, None] == jnp.arange(tap_count, dtype=jnp.int32)[None, None, :]) & live_slots[:, :, None]
    onehot = jnp.where(matches, 1.0, 0.0).astype(jnp.float32)
    legendre = legendre_table(jnp.arange(M, dtype=jnp.int32), NLAT, L)
    weighted = legendre * quad_weights(NLAT)[None, None, :]
    all_modes = jnp.arange(M, dtype=jnp.int32)
    cosine, sine_val = trig_table(all_modes, jnp.arange(NLON, dtype=jnp.int32), NLON)
    factor = jnp.where(all_modes == 0, 1.0, 2.0).astype(jnp.float32)[:, None]
    for block in range(BLOCKS):
        normed = layer_norm(state, norm_gain[block, 0]).astype(jnp.bfloat16)
        kernel = jnp.einsum('ist,isk->itk', onehot, disco_kernel[block], precision=exact_prec)
        padded = jnp.pad(normed, ((1, 1), (0, 0), (0, 0)))

        def disco_row(packed):
            row_idx, kernel_row = packed
            window = lax.dynamic_slice_in_dim(padded, row_idx, 3, 0)
            stacked = jnp.stack([jnp.roll(window[tap_id // tap_span], R - tap_id % tap_span, axis=0) for tap_id in range(tap_count)])
            conv_row = jnp.einsum('tk,tpc->pkc', kernel_row, stacked.astype(jnp.float32), precision=exact_prec).astype(jnp.bfloat16)
            return jnp.dot(conv_row.reshape(NLON, K * C), disco_mix[block], preferred_element_type=jnp.float32)
        disco_out = lax.map(disco_row, (jnp.arange(NLAT, dtype=jnp.int32), kernel))
        as_float = normed.astype(jnp.float32)

        def add_slab(total, slab_idx):
            start = (slab_idx * slab_width).astype(jnp.int32)
            slab_field = lax.dynamic_slice_in_dim(as_float, start, slab_width, 1)
            slab_cos = lax.dynamic_slice_in_dim(cosine, start, slab_width, 1)
            slab_sin = lax.dynamic_slice_in_dim(sine_val, start, slab_width, 1)
            real_part = jnp.einsum('mp,ipc->mic', slab_cos / NLON, slab_field, precision=exact_prec)
            imag_part = jnp.einsum('mp,ipc->mic', -slab_sin / NLON, slab_field, precision=exact_prec)
            rounded = lax.optimization_barrier(jnp.stack([real_part, imag_part], axis=2).astype(jnp.bfloat16))
            return (total + rounded.astype(jnp.float32), None)
        blank_spec = jnp.zeros((M, NLAT, 2, C), jnp.float32)
        spectrum, unused = lax.scan(add_slab, blank_spec, jnp.arange(SLABS, dtype=jnp.int32))
        gains = filter_gain[block]

        def filter_mode(packed):
            legendre_m, weighted_m, spectrum_m = packed
            coefficient = jnp.einsum('lj,jrc->lrc', weighted_m, spectrum_m, precision=exact_prec)
            scaled = coefficient * gains[:, None, :]
            return jnp.einsum('lj,lrc->jrc', legendre_m, scaled, precision=exact_prec).astype(jnp.bfloat16)
        filtered = lax.map(filter_mode, (legendre, weighted, spectrum))
        restored = filtered.astype(jnp.float32)
        spectral_out = jnp.einsum('mp,mic->ipc', factor * cosine, restored[:, :, 0], precision=exact_prec) - jnp.einsum('mp,mic->ipc', factor * sine_val, restored[:, :, 1], precision=exact_prec)
        state = state + disco_out + spectral_out
        normed_two = layer_norm(state, norm_gain[block, 1]).astype(jnp.bfloat16)
        hidden = jax.nn.gelu(jnp.dot(normed_two, mlp_in[block], preferred_element_type=jnp.float32)).astype(jnp.bfloat16)
        state = state + jnp.dot(hidden, mlp_out[block], preferred_element_type=jnp.float32)
    return state
```

```python
import functools
import math

import jax
import jax.numpy as jnp
from jax import lax
from jax.experimental import pallas as pl
from jax.experimental.pallas import tpu as pltpu
from jax.sharding import PartitionSpec as P

M = 256
L = 256
K = 8
R = 8
S = 24
WIDTH = 64
REACH = WIDTH + 2 * R
LANES = 256

exact_prec = lax.Precision.HIGHEST


def halo(cells, axis, dim, width, closed):
    count = lax.axis_size(axis)
    ends = count if closed else count - 1
    head = lax.slice_in_dim(cells, 0, width, axis=dim)
    tail = lax.slice_in_dim(cells, cells.shape[dim] - width, cells.shape[dim], axis=dim)
    before = lax.ppermute(tail, axis, [(i, (i + 1) % count) for i in range(ends)])
    after = lax.ppermute(head, axis, [((i + 1) % count, i) for i in range(ends)])
    return before, after


def layer_norm(values, gain):
    center = values - jnp.mean(values, axis=-1, keepdims=True)
    spread = jnp.mean(center * center, axis=-1, keepdims=True)
    return center * lax.rsqrt(spread + 1e-05) * gain


def trig_table(mode_ids, lon_points, lon_total):
    product = mode_ids * lon_points % lon_total
    angles = product.astype(jnp.float32) * (2.0 * math.pi / lon_total)
    return (jnp.cos(angles), jnp.sin(angles))


def colatitudes(lat_count):
    row_ids = jnp.arange(lat_count).astype(jnp.float32)
    return math.pi * (row_ids + 0.5) / lat_count


def legendre_kernel(orders_ref, cosine_ref, diagonal_ref, out_ref):
    orders = orders_ref[...]
    cosine = cosine_ref[...]
    diagonal = diagonal_ref[...]
    ord_sq = orders * orders
    second_coef = cosine * jnp.sqrt(2.0 * orders + 3.0)

    def advance(step, carry):
        latest, earlier = carry
        degree = step.astype(jnp.float32)
        deg_sq = degree * degree
        upper_coef = jnp.sqrt((4.0 * deg_sq - 1.0) / jnp.maximum(deg_sq - ord_sq, 1.0))
        previous = degree - 1.0
        lower_coef = jnp.sqrt(
            jnp.maximum(previous * previous - ord_sq, 0.0)
            / jnp.maximum(4.0 * previous * previous - 1.0, 1.0)
        )
        recurred = upper_coef * (cosine * latest - lower_coef * earlier)
        current = jnp.where(
            degree < orders,
            0.0,
            jnp.where(
                degree == orders,
                diagonal,
                jnp.where(degree == orders + 1.0, second_coef * latest, recurred),
            ),
        )
        out_ref[step] = current
        return current, latest

    blank = diagonal * 0.0
    lax.fori_loop(0, out_ref.shape[0], advance, (blank, blank), unroll=8)


def legendre_table(mode_ids, lat_count, degrees):
    colatitude = colatitudes(lat_count)
    cosine = jnp.cos(colatitude)[None, :]
    sine_val = jnp.sin(colatitude)[None, :]
    orders = mode_ids.astype(jnp.float32)[:, None]
    factor_ids = jnp.arange(1, degrees + 1).astype(jnp.float32)[None, :]
    log_terms = jnp.where(
        factor_ids <= orders, 0.5 * jnp.log((2.0 * factor_ids - 1.0) / (2.0 * factor_ids)), 0.0
    )
    log_start = 0.5 * jnp.log((2.0 * orders + 1.0) / (4.0 * math.pi)) + jnp.sum(
        log_terms, axis=1, keepdims=True
    )
    diagonal = jnp.exp(log_start + orders * jnp.log(sine_val))
    shape = diagonal.shape
    return pl.pallas_call(
        legendre_kernel,
        out_shape=jax.ShapeDtypeStruct((degrees,) + shape, jnp.float32),
        compiler_params=pltpu.CompilerParams(vmem_limit_bytes=48 * 2**20),
        cost_estimate=pl.CostEstimate(
            flops=40 * degrees * 1024, bytes_accessed=4 * degrees * 2048, transcendentals=0
        ),
        name="legendre",
    )(jnp.broadcast_to(orders, shape), jnp.broadcast_to(cosine, shape), diagonal)


def disco_body(above_ref, here_ref, below_ref, base_ref, mix_ref, state_ref, out_ref, band_ref):
    cols = state_ref.shape[1]
    channels = state_ref.shape[2]
    for k in range(K):
        row = jnp.broadcast_to(base_ref[0, k : k + 1, :], (WIDTH, LANES))
        band = pltpu.roll(row, 0, 1, stride=1, stride_axis=0)
        band_ref[k * WIDTH : (k + 1) * WIDTH, :] = band.astype(jnp.bfloat16)
    band = band_ref[:, : 3 * REACH]
    pieces = []
    for start in range(0, cols, WIDTH):
        window = jnp.concatenate(
            [ref[0, start : start + REACH, :] for ref in (above_ref, here_ref, below_ref)], axis=0
        )
        conv = jnp.dot(band, window, preferred_element_type=jnp.float32).astype(jnp.bfloat16)
        pieces.append(
            jnp.concatenate([conv[k * WIDTH : (k + 1) * WIDTH] for k in range(K)], axis=1)
        )
    mixed = jnp.dot(
        jnp.concatenate(pieces, axis=0), mix_ref[...], preferred_element_type=jnp.float32
    )
    out_ref[0] = state_ref[0] + mixed[:cols]


def disco_update(extended, base, mix, state):
    rows, cols, channels = state.shape
    width = extended.shape[1]

    def ext_spec(offset):
        return pl.BlockSpec((1, width, channels), lambda i: (i + offset, 0, 0))

    cell = pl.BlockSpec((1, cols, channels), lambda i: (i, 0, 0))
    return pl.pallas_call(
        disco_body,
        grid=(rows,),
        in_specs=[
            ext_spec(0),
            ext_spec(1),
            ext_spec(2),
            pl.BlockSpec((1, K, LANES), lambda i: (i, 0, 0)),
            pl.BlockSpec(mix.shape, lambda i: (0, 0)),
            cell,
        ],
        out_specs=cell,
        out_shape=jax.ShapeDtypeStruct(state.shape, jnp.float32),
        scratch_shapes=[pltpu.VMEM((K * WIDTH, LANES), jnp.bfloat16)],
        compiler_params=pltpu.CompilerParams(vmem_limit_bytes=48 * 2**20),
        cost_estimate=pl.CostEstimate(
            flops=2 * rows * cols * K * channels * 512, bytes_accessed=12 * 2**20, transcendentals=0
        ),
        name="disco",
    )(extended, extended, extended, base, mix, state)


def mlp_body(state_ref, spectral_ref, gain_ref, in_ref, out_mat_ref, out_ref):
    state = state_ref[0] + spectral_ref[0].astype(jnp.float32)
    normed = layer_norm(state, gain_ref[...]).astype(jnp.bfloat16)
    hidden = jax.nn.gelu(jnp.dot(normed, in_ref[...], preferred_element_type=jnp.float32))
    out_ref[0] = state + jnp.dot(
        hidden.astype(jnp.bfloat16), out_mat_ref[...], preferred_element_type=jnp.float32
    )


def mlp_update(state, spectral, gain, mat_in, mat_out):
    rows, cols, channels = state.shape
    cell = pl.BlockSpec((1, cols, channels), lambda i: (i, 0, 0))
    return pl.pallas_call(
        mlp_body,
        grid=(rows,),
        in_specs=[
            cell,
            cell,
            pl.BlockSpec(gain.shape, lambda i: (0, 0)),
            pl.BlockSpec(mat_in.shape, lambda i: (0, 0)),
            pl.BlockSpec(mat_out.shape, lambda i: (0, 0)),
        ],
        out_specs=cell,
        out_shape=jax.ShapeDtypeStruct(state.shape, jnp.float32),
        compiler_params=pltpu.CompilerParams(vmem_limit_bytes=48 * 2**20),
        name="mlp",
    )(state, spectral, gain, mat_in, mat_out)


def local(state, norm_gain, disco_kernel, taps, counts, disco_mix, filter_gain, mlp_in, mlp_out):
    lat_rows, lon_cols, channels = state.shape
    lon_parts = lax.axis_size("lon")
    lat_parts = lax.axis_size("lat")
    parts = lon_parts * lat_parts
    lon_total = lon_cols * lon_parts
    lat_total = lat_rows * lat_parts
    rank = lax.axis_index("lat") * lon_parts + lax.axis_index("lon")
    modes_own = M // parts
    tap_span = 2 * R + 1

    normed = layer_norm(state, norm_gain[0, 0]).astype(jnp.bfloat16)
    whole_rows = lax.all_to_all(normed, "lon", split_axis=0, concat_axis=1, tiled=True)

    slot_ids = jnp.arange(2 * M, dtype=jnp.int32)
    imaginary = slot_ids // modes_own % 2 == 1
    slot_modes = slot_ids // (2 * modes_own) * modes_own + slot_ids % modes_own
    points = jnp.arange(lon_total, dtype=jnp.int32)
    cosine, sine_val = trig_table(slot_modes[:, None], points[None, :], lon_total)
    analysis = (jnp.where(imaginary[:, None], -sine_val, cosine) / lon_total).astype(jnp.bfloat16)
    factor = jnp.where(slot_modes == 0, 1.0, 2.0).astype(jnp.float32)
    cosine, sine_val = trig_table(slot_modes[None, :], points[:, None], lon_total)
    synthesis = (jnp.where(imaginary[None, :], -sine_val, cosine) * factor[None, :]).astype(
        jnp.bfloat16
    )

    own_modes = rank * modes_own + jnp.arange(modes_own, dtype=jnp.int32)
    legendre = legendre_table(own_modes, lat_total, L)
    weights = math.pi * jnp.sin(colatitudes(lat_total)) / lat_total
    weighted = (legendre * weights[None, None, :]).astype(jnp.bfloat16)
    legendre = legendre.astype(jnp.bfloat16)

    live = jnp.arange(S, dtype=jnp.int32)[None, :] < counts[:, None]
    lanes = taps // tap_span * REACH + taps % tap_span
    matches = (lanes[:, :, None] == jnp.arange(LANES, dtype=jnp.int32)) & live[:, :, None]
    base = jnp.einsum(
        "isq,isk->ikq", matches.astype(jnp.float32), disco_kernel[0], precision=exact_prec
    )

    above, below = halo(normed, "lat", 0, 1, False)
    extended = jnp.concatenate([above, normed, below], axis=0)
    west, east = halo(extended, "lon", 1, R, True)
    blocks = -(-lon_cols // WIDTH)
    spare = blocks * WIDTH - lon_cols
    extended = jnp.concatenate(
        [west, extended, east, jnp.zeros((lat_rows + 2, spare, channels), jnp.bfloat16)], axis=1
    )
    partial = disco_update(extended, base, disco_mix[0], state)

    spectrum = jnp.einsum(
        "mp,ipc->imc", analysis, whole_rows, preferred_element_type=jnp.float32
    ).astype(jnp.bfloat16)
    owned = lax.all_to_all(spectrum, ("lat", "lon"), split_axis=1, concat_axis=0, tiled=True)
    owned = owned.reshape(lat_total, 2, modes_own, channels)
    coefficient = jnp.einsum(
        "lmj,jrmc->mlrc", weighted, owned, preferred_element_type=jnp.float32
    )
    scaled = (coefficient * filter_gain[0][None, :, None, :]).astype(jnp.bfloat16)
    filtered = jnp.einsum(
        "lmj,mlrc->mjrc", legendre, scaled, preferred_element_type=jnp.float32
    ).astype(jnp.bfloat16)
    filtered = jnp.transpose(filtered, (1, 2, 0, 3)).reshape(
        lat_total, 2 * modes_own, channels
    )
    returned = lax.all_to_all(filtered, ("lat", "lon"), split_axis=0, concat_axis=1, tiled=True)
    spectral = jnp.einsum(
        "pm,imc->ipc", synthesis, returned, preferred_element_type=jnp.float32
    ).astype(jnp.bfloat16)
    spectral = lax.all_to_all(spectral, "lon", split_axis=1, concat_axis=0, tiled=True)
    return mlp_update(partial, spectral, norm_gain[0, 1:2], mlp_in[0], mlp_out[0])


def solution(mesh):
    in_specs = (
        P(("grp", "lat"), "lon", None),
        P(),
        P(None, "lat", None, None),
        P("lat", None),
        P("lat"),
        P(),
        P(),
        P(),
        P(),
    )
    out_specs = P(("grp", "lat"), "lon", None)
    return jax.shard_map(local, mesh=mesh, in_specs=in_specs, out_specs=out_specs, check_vma=False)
```

```python
import functools
import math

import jax
import jax.numpy as jnp
from jax import lax
from jax.experimental import pallas as pl
from jax.experimental.pallas import tpu as pltpu
from jax.sharding import PartitionSpec as P

M = 256
L = 256
K = 8
R = 8
S = 24
WIDTH = 64
REACH = WIDTH + 2 * R
LANES = 256
STEP = 30
CUTS = 2

exact_prec = lax.Precision.HIGHEST


def halo(cells, axis, dim, width, closed):
    count = lax.axis_size(axis)
    ends = count if closed else count - 1
    head = lax.slice_in_dim(cells, 0, width, axis=dim)
    tail = lax.slice_in_dim(cells, cells.shape[dim] - width, cells.shape[dim], axis=dim)
    before = lax.ppermute(tail, axis, [(i, (i + 1) % count) for i in range(ends)])
    after = lax.ppermute(head, axis, [((i + 1) % count, i) for i in range(ends)])
    return before, after


def layer_norm(values, gain):
    center = values - jnp.mean(values, axis=-1, keepdims=True)
    spread = jnp.mean(center * center, axis=-1, keepdims=True)
    return center * lax.rsqrt(spread + 1e-05) * gain


def trig_table(mode_ids, lon_points, lon_total):
    product = mode_ids * lon_points % lon_total
    angles = product.astype(jnp.float32) * (2.0 * math.pi / lon_total)
    return (jnp.cos(angles), jnp.sin(angles))


def colatitudes(lat_count):
    row_ids = jnp.arange(lat_count).astype(jnp.float32)
    return math.pi * (row_ids + 0.5) / lat_count


def legendre_kernel(orders_ref, cosine_ref, diagonal_ref, out_ref):
    orders = orders_ref[...]
    cosine = cosine_ref[...]
    diagonal = diagonal_ref[...]
    ord_sq = orders * orders
    second_coef = cosine * jnp.sqrt(2.0 * orders + 3.0)

    def advance(step, carry):
        latest, earlier = carry
        degree = step.astype(jnp.float32)
        deg_sq = degree * degree
        upper_coef = jnp.sqrt((4.0 * deg_sq - 1.0) / jnp.maximum(deg_sq - ord_sq, 1.0))
        previous = degree - 1.0
        lower_coef = jnp.sqrt(
            jnp.maximum(previous * previous - ord_sq, 0.0)
            / jnp.maximum(4.0 * previous * previous - 1.0, 1.0)
        )
        recurred = upper_coef * (cosine * latest - lower_coef * earlier)
        current = jnp.where(
            degree < orders,
            0.0,
            jnp.where(
                degree == orders,
                diagonal,
                jnp.where(degree == orders + 1.0, second_coef * latest, recurred),
            ),
        )
        out_ref[step] = current
        return current, latest

    blank = diagonal * 0.0
    lax.fori_loop(0, out_ref.shape[0], advance, (blank, blank), unroll=8)


def legendre_table(mode_ids, lat_count, degrees):
    colatitude = colatitudes(lat_count)
    cosine = jnp.cos(colatitude)[None, :]
    sine_val = jnp.sin(colatitude)[None, :]
    orders = mode_ids.astype(jnp.float32)[:, None]
    factor_ids = jnp.arange(1, degrees + 1).astype(jnp.float32)[None, :]
    log_terms = jnp.where(
        factor_ids <= orders, 0.5 * jnp.log((2.0 * factor_ids - 1.0) / (2.0 * factor_ids)), 0.0
    )
    log_start = 0.5 * jnp.log((2.0 * orders + 1.0) / (4.0 * math.pi)) + jnp.sum(
        log_terms, axis=1, keepdims=True
    )
    diagonal = jnp.exp(log_start + orders * jnp.log(sine_val))
    shape = diagonal.shape
    return pl.pallas_call(
        legendre_kernel,
        out_shape=jax.ShapeDtypeStruct((degrees,) + shape, jnp.float32),
        compiler_params=pltpu.CompilerParams(vmem_limit_bytes=48 * 2**20),
        cost_estimate=pl.CostEstimate(
            flops=40 * degrees * 1024, bytes_accessed=4 * degrees * 2048, transcendentals=0
        ),
        name="legendre",
    )(jnp.broadcast_to(orders, shape), jnp.broadcast_to(cosine, shape), diagonal)


def disco_body(above_ref, here_ref, below_ref, base_ref, mix_ref, out_ref, band_ref):
    cols = out_ref.shape[1]
    for k in range(K):
        row = jnp.broadcast_to(base_ref[0, k : k + 1, :], (WIDTH, LANES))
        band = pltpu.roll(row, 0, 1, stride=1, stride_axis=0)
        band_ref[k * WIDTH : (k + 1) * WIDTH, :] = band.astype(jnp.bfloat16)
    band = band_ref[:, : 3 * REACH]
    pieces = []
    for start in range(0, cols, WIDTH):
        window = jnp.concatenate(
            [ref[0, start : start + REACH, :] for ref in (above_ref, here_ref, below_ref)], axis=0
        )
        conv = jnp.dot(band, window, preferred_element_type=jnp.float32).astype(jnp.bfloat16)
        pieces.append(
            jnp.concatenate([conv[k * WIDTH : (k + 1) * WIDTH] for k in range(K)], axis=1)
        )
    mixed = jnp.dot(
        jnp.concatenate(pieces, axis=0), mix_ref[...], preferred_element_type=jnp.float32
    )
    out_ref[0] = mixed[:cols]


def disco_update(extended, base, mix, cols):
    rows = base.shape[0]
    width, channels = extended.shape[1:]

    def ext_spec(offset):
        return pl.BlockSpec((1, width, channels), lambda i: (i + offset, 0, 0))

    cell = pl.BlockSpec((1, cols, channels), lambda i: (i, 0, 0))
    return pl.pallas_call(
        disco_body,
        grid=(rows,),
        in_specs=[
            ext_spec(0),
            ext_spec(1),
            ext_spec(2),
            pl.BlockSpec((1, K, LANES), lambda i: (i, 0, 0)),
            pl.BlockSpec(mix.shape, lambda i: (0, 0)),
        ],
        out_specs=cell,
        out_shape=jax.ShapeDtypeStruct((rows, cols, channels), jnp.float32),
        scratch_shapes=[pltpu.VMEM((K * WIDTH, LANES), jnp.bfloat16)],
        compiler_params=pltpu.CompilerParams(vmem_limit_bytes=48 * 2**20),
        cost_estimate=pl.CostEstimate(
            flops=2 * rows * cols * K * channels * 512, bytes_accessed=12 * 2**20, transcendentals=0
        ),
        name="disco",
    )(extended, extended, extended, base, mix)


def mlp_body(state_ref, disco_ref, *refs):
    *spectral_refs, gain_ref, in_ref, out_mat_ref, out_ref = refs
    cells = state_ref.shape[0] * state_ref.shape[1]
    channels = state_ref.shape[2]
    spectral = jnp.concatenate([ref[...].astype(jnp.float32) for ref in spectral_refs], axis=2)
    state = (state_ref[...] + disco_ref[...] + spectral).reshape(cells, channels)
    normed = layer_norm(state, gain_ref[...]).astype(jnp.bfloat16)
    hidden = jax.nn.gelu(jnp.dot(normed, in_ref[...], preferred_element_type=jnp.float32))
    state = state + jnp.dot(
        hidden.astype(jnp.bfloat16), out_mat_ref[...], preferred_element_type=jnp.float32
    )
    out_ref[...] = state.reshape(out_ref.shape)


def mlp_update(state, disco, spectral, gain, mat_in, mat_out):
    cols, rows, channels = state.shape
    step = max(size for size in range(1, STEP + 1) if cols % size == 0)
    cell = pl.BlockSpec((step, rows, channels), lambda i: (i, 0, 0))
    return pl.pallas_call(
        mlp_body,
        grid=(cols // step,),
        in_specs=[cell, cell]
        + [pl.BlockSpec((step, rows, part.shape[2]), lambda i: (i, 0, 0)) for part in spectral]
        + [pl.BlockSpec(mat.shape, lambda i: (0, 0)) for mat in (gain, mat_in, mat_out)],
        out_specs=cell,
        out_shape=jax.ShapeDtypeStruct(state.shape, jnp.float32),
        compiler_params=pltpu.CompilerParams(vmem_limit_bytes=48 * 2**20),
        name="mlp",
    )(state, disco, *spectral, gain, mat_in, mat_out)


def local(state, norm_gain, disco_kernel, taps, counts, disco_mix, filter_gain, mlp_in, mlp_out):
    lat_rows, lon_cols, channels = state.shape
    lon_parts = lax.axis_size("lon")
    lat_parts = lax.axis_size("lat")
    parts = lon_parts * lat_parts
    lon_total = lon_cols * lon_parts
    lat_total = lat_rows * lat_parts
    rank = lax.axis_index("lat") * lon_parts + lax.axis_index("lon")
    modes_own = M // parts
    tap_span = 2 * R + 1

    normed = layer_norm(state, norm_gain[0, 0]).astype(jnp.bfloat16)
    cut = channels // CUTS
    whole_rows = [
        lax.all_to_all(
            normed[:, :, n * cut : (n + 1) * cut], "lon", split_axis=0, concat_axis=1, tiled=True
        )
        for n in range(CUTS)
    ]

    slot_ids = jnp.arange(2 * M, dtype=jnp.int32)
    imaginary = slot_ids // modes_own % 2 == 1
    slot_modes = slot_ids // (2 * modes_own) * modes_own + slot_ids % modes_own
    points = jnp.arange(lon_total, dtype=jnp.int32)
    cosine, sine_val = trig_table(slot_modes[:, None], points[None, :], lon_total)
    analysis = (jnp.where(imaginary[:, None], -sine_val, cosine) / lon_total).astype(jnp.bfloat16)
    factor = jnp.where(slot_modes == 0, 1.0, 2.0).astype(jnp.float32)
    cosine, sine_val = trig_table(slot_modes[None, :], points[:, None], lon_total)
    synthesis = (jnp.where(imaginary[None, :], -sine_val, cosine) * factor[None, :]).astype(
        jnp.bfloat16
    )

    own_modes = rank * modes_own + jnp.arange(modes_own, dtype=jnp.int32)
    legendre = legendre_table(own_modes, lat_total, L)
    weights = math.pi * jnp.sin(colatitudes(lat_total)) / lat_total
    weighted = (legendre * weights[None, None, :]).astype(jnp.bfloat16)
    legendre = legendre.astype(jnp.bfloat16)

    live = jnp.arange(S, dtype=jnp.int32)[None, :] < counts[:, None]
    lanes = taps // tap_span * REACH + taps % tap_span
    matches = (lanes[:, :, None] == jnp.arange(LANES, dtype=jnp.int32)) & live[:, :, None]
    base = jnp.einsum(
        "isq,isk->ikq", matches.astype(jnp.float32), disco_kernel[0], precision=exact_prec
    )

    above, below = halo(normed, "lat", 0, 1, False)
    extended = jnp.concatenate([above, normed, below], axis=0)
    west, east = halo(extended, "lon", 1, R, True)
    blocks = -(-lon_cols // WIDTH)
    spare = blocks * WIDTH - lon_cols
    extended = jnp.concatenate(
        [west, extended, east, jnp.zeros((lat_rows + 2, spare, channels), jnp.bfloat16)], axis=1
    )
    disco = jnp.transpose(disco_update(extended, base, disco_mix[0], lon_cols), (1, 0, 2))

    spectral = []
    for n in range(CUTS):
        gain = filter_gain[0, :, n * cut : (n + 1) * cut]
        spectrum = jnp.einsum(
            "mp,ipc->imc", analysis, whole_rows[n], preferred_element_type=jnp.float32
        ).astype(jnp.bfloat16)
        owned = lax.all_to_all(spectrum, ("lat", "lon"), split_axis=1, concat_axis=0, tiled=True)
        owned = owned.reshape(lat_total, 2, modes_own, cut)
        coefficient = jnp.einsum(
            "lmj,jrmc->mlrc", weighted, owned, preferred_element_type=jnp.float32
        )
        scaled = (coefficient * gain[None, :, None, :]).astype(jnp.bfloat16)
        filtered = jnp.einsum(
            "lmj,mlrc->mjrc", legendre, scaled, preferred_element_type=jnp.float32
        ).astype(jnp.bfloat16)
        filtered = jnp.transpose(filtered, (1, 2, 0, 3)).reshape(lat_total, 2 * modes_own, cut)
        returned = lax.all_to_all(
            filtered, ("lat", "lon"), split_axis=0, concat_axis=1, tiled=True
        )
        restored = jnp.einsum(
            "pm,imc->ipc", synthesis, returned, preferred_element_type=jnp.float32
        ).astype(jnp.bfloat16)
        restored = lax.all_to_all(restored, "lon", split_axis=1, concat_axis=0, tiled=True)
        spectral.append(jnp.transpose(restored, (1, 0, 2)))
    result = mlp_update(
        jnp.transpose(state, (1, 0, 2)), disco, spectral, norm_gain[0, 1:2], mlp_in[0], mlp_out[0]
    )
    return jnp.transpose(result, (1, 0, 2))


def solution(mesh):
    in_specs = (
        P(("grp", "lat"), "lon", None),
        P(),
        P(None, "lat", None, None),
        P("lat", None),
        P("lat"),
        P(),
        P(),
        P(),
        P(),
    )
    out_specs = P(("grp", "lat"), "lon", None)
    return jax.shard_map(local, mesh=mesh, in_specs=in_specs, out_specs=out_specs, check_vma=False)
```

```python
import math

import jax
import jax.numpy as jnp
from jax import lax
from jax.experimental import pallas as pl
from jax.experimental.pallas import tpu as pltpu
from jax.sharding import PartitionSpec as P

M = 256
L = 256
K = 8
R = 8
S = 24
WIDTH = 64
REACH = WIDTH + 2 * R
LANES = 256
STEP = 30
CUTS = 1

exact_prec = lax.Precision.HIGHEST


def halo(cells, axis, dim, width, closed):
    count = lax.axis_size(axis)
    ends = count if closed else count - 1
    head = lax.slice_in_dim(cells, 0, width, axis=dim)
    tail = lax.slice_in_dim(cells, cells.shape[dim] - width, cells.shape[dim], axis=dim)
    before = lax.ppermute(tail, axis, [(i, (i + 1) % count) for i in range(ends)])
    after = lax.ppermute(head, axis, [((i + 1) % count, i) for i in range(ends)])
    return before, after


def layer_norm(values, gain):
    center = values - jnp.mean(values, axis=-1, keepdims=True)
    spread = jnp.mean(center * center, axis=-1, keepdims=True)
    return center * lax.rsqrt(spread + 1e-05) * gain


def colatitudes(lat_count):
    row_ids = jnp.arange(lat_count).astype(jnp.float32)
    return math.pi * (row_ids + 0.5) / lat_count


def legendre_kernel(orders_ref, cosine_ref, diagonal_ref, out_ref):
    orders = orders_ref[...]
    cosine = cosine_ref[...]
    diagonal = diagonal_ref[...]
    ord_sq = orders * orders
    second_coef = cosine * jnp.sqrt(2.0 * orders + 3.0)

    def advance(step, carry):
        latest, earlier = carry
        degree = step.astype(jnp.float32)
        deg_sq = degree * degree
        upper_coef = jnp.sqrt((4.0 * deg_sq - 1.0) / jnp.maximum(deg_sq - ord_sq, 1.0))
        previous = degree - 1.0
        lower_coef = jnp.sqrt(
            jnp.maximum(previous * previous - ord_sq, 0.0)
            / jnp.maximum(4.0 * previous * previous - 1.0, 1.0)
        )
        recurred = upper_coef * (cosine * latest - lower_coef * earlier)
        current = jnp.where(
            degree < orders,
            0.0,
            jnp.where(
                degree == orders,
                diagonal,
                jnp.where(degree == orders + 1.0, second_coef * latest, recurred),
            ),
        )
        out_ref[step] = current
        return current, latest

    blank = diagonal * 0.0
    lax.fori_loop(0, out_ref.shape[0], advance, (blank, blank), unroll=8)


def legendre_table(mode_ids, lat_count, degrees):
    colatitude = colatitudes(lat_count)
    cosine = jnp.cos(colatitude)[None, :]
    sine_val = jnp.sin(colatitude)[None, :]
    orders = mode_ids.astype(jnp.float32)[:, None]
    factor_ids = jnp.arange(1, degrees + 1).astype(jnp.float32)[None, :]
    log_terms = jnp.where(
        factor_ids <= orders, 0.5 * jnp.log((2.0 * factor_ids - 1.0) / (2.0 * factor_ids)), 0.0
    )
    log_start = 0.5 * jnp.log((2.0 * orders + 1.0) / (4.0 * math.pi)) + jnp.sum(
        log_terms, axis=1, keepdims=True
    )
    diagonal = jnp.exp(log_start + orders * jnp.log(sine_val))
    shape = diagonal.shape
    return pl.pallas_call(
        legendre_kernel,
        out_shape=jax.ShapeDtypeStruct((degrees,) + shape, jnp.float32),
        compiler_params=pltpu.CompilerParams(vmem_limit_bytes=48 * 2**20),
        cost_estimate=pl.CostEstimate(
            flops=40 * degrees * 1024, bytes_accessed=4 * degrees * 2048, transcendentals=0
        ),
        name="legendre",
    )(jnp.broadcast_to(orders, shape), jnp.broadcast_to(cosine, shape), diagonal)


def disco_body(above_ref, here_ref, below_ref, base_ref, mix_ref, out_ref, band_ref):
    cols = out_ref.shape[1]
    for k in range(K):
        row = jnp.broadcast_to(base_ref[0, k : k + 1, :], (WIDTH, LANES))
        band = pltpu.roll(row, 0, 1, stride=1, stride_axis=0)
        band_ref[k * WIDTH : (k + 1) * WIDTH, :] = band.astype(jnp.bfloat16)
    band = band_ref[:, : 3 * REACH]
    pieces = []
    for start in range(0, cols, WIDTH):
        window = jnp.concatenate(
            [ref[0, start : start + REACH, :] for ref in (above_ref, here_ref, below_ref)], axis=0
        )
        conv = jnp.dot(band, window, preferred_element_type=jnp.float32).astype(jnp.bfloat16)
        pieces.append(
            jnp.concatenate([conv[k * WIDTH : (k + 1) * WIDTH] for k in range(K)], axis=1)
        )
    mixed = jnp.dot(
        jnp.concatenate(pieces, axis=0), mix_ref[...], preferred_element_type=jnp.float32
    )
    out_ref[0] = mixed[:cols]


def disco_update(extended, base, mix, cols):
    rows = base.shape[0]
    width, channels = extended.shape[1:]

    def ext_spec(offset):
        return pl.BlockSpec((1, width, channels), lambda i: (i + offset, 0, 0))

    cell = pl.BlockSpec((1, cols, channels), lambda i: (i, 0, 0))
    return pl.pallas_call(
        disco_body,
        grid=(rows,),
        in_specs=[
            ext_spec(0),
            ext_spec(1),
            ext_spec(2),
            pl.BlockSpec((1, K, LANES), lambda i: (i, 0, 0)),
            pl.BlockSpec(mix.shape, lambda i: (0, 0)),
        ],
        out_specs=cell,
        out_shape=jax.ShapeDtypeStruct((rows, cols, channels), jnp.float32),
        scratch_shapes=[pltpu.VMEM((K * WIDTH, LANES), jnp.bfloat16)],
        compiler_params=pltpu.CompilerParams(vmem_limit_bytes=48 * 2**20),
        cost_estimate=pl.CostEstimate(
            flops=2 * rows * cols * K * channels * 512, bytes_accessed=12 * 2**20, transcendentals=0
        ),
        name="disco",
    )(extended, extended, extended, base, mix)


def mlp_body(state_ref, disco_ref, *refs):
    *spectral_refs, gain_ref, in_ref, out_mat_ref, out_ref = refs
    cells = state_ref.shape[0] * state_ref.shape[1]
    channels = state_ref.shape[2]
    spectral = jnp.concatenate([ref[...].astype(jnp.float32) for ref in spectral_refs], axis=2)
    state = (state_ref[...] + disco_ref[...] + spectral).reshape(cells, channels)
    normed = layer_norm(state, gain_ref[...]).astype(jnp.bfloat16)
    hidden = jax.nn.gelu(jnp.dot(normed, in_ref[...], preferred_element_type=jnp.float32))
    state = state + jnp.dot(
        hidden.astype(jnp.bfloat16), out_mat_ref[...], preferred_element_type=jnp.float32
    )
    out_ref[...] = state.reshape(out_ref.shape)


def mlp_update(state, disco, spectral, gain, mat_in, mat_out):
    cols, rows, channels = state.shape
    step = max(size for size in range(1, STEP + 1) if cols % size == 0)
    cell = pl.BlockSpec((step, rows, channels), lambda i: (i, 0, 0))
    return pl.pallas_call(
        mlp_body,
        grid=(cols // step,),
        in_specs=[cell, cell]
        + [pl.BlockSpec((step, rows, part.shape[2]), lambda i: (i, 0, 0)) for part in spectral]
        + [pl.BlockSpec(mat.shape, lambda i: (0, 0)) for mat in (gain, mat_in, mat_out)],
        out_specs=cell,
        out_shape=jax.ShapeDtypeStruct(state.shape, jnp.float32),
        compiler_params=pltpu.CompilerParams(vmem_limit_bytes=48 * 2**20),
        name="mlp",
    )(state, disco, *spectral, gain, mat_in, mat_out)


def local(state, norm_gain, disco_kernel, taps, counts, disco_mix, filter_gain, mlp_in, mlp_out):
    lat_rows, lon_cols, channels = state.shape
    lon_parts = lax.axis_size("lon")
    lat_parts = lax.axis_size("lat")
    parts = lon_parts * lat_parts
    lon_total = lon_cols * lon_parts
    lat_total = lat_rows * lat_parts
    rank = lax.axis_index("lat") * lon_parts + lax.axis_index("lon")
    modes_own = M // parts
    tap_span = 2 * R + 1

    normed = layer_norm(state, norm_gain[0, 0]).astype(jnp.bfloat16)
    slot_ids = jnp.arange(2 * M, dtype=jnp.int32)
    imaginary = slot_ids // modes_own % 2 == 1
    slot_modes = slot_ids // (2 * modes_own) * modes_own + slot_ids % modes_own
    points = jnp.arange(lon_total, dtype=jnp.int32)
    normed, slot_modes = lax.optimization_barrier((normed, slot_modes))
    cut = channels // CUTS
    whole_rows = [
        lax.all_to_all(
            normed[:, :, n * cut : (n + 1) * cut], "lon", split_axis=0, concat_axis=1, tiled=True
        )
        for n in range(CUTS)
    ]
    quarter = jnp.where(imaginary, lon_total // 4, 0)
    steps = (slot_modes[:, None] * points[None, :] + quarter[:, None]) % lon_total
    waves = jnp.cos(steps.astype(jnp.float32) * (2.0 * math.pi / lon_total)).astype(jnp.bfloat16)
    waves = lax.optimization_barrier(waves)

    own_modes = rank * modes_own + jnp.arange(modes_own, dtype=jnp.int32)
    factor = jnp.where(own_modes == 0, 1.0, 2.0).astype(jnp.float32)
    legendre = legendre_table(own_modes, lat_total, L)
    weights = math.pi * jnp.sin(colatitudes(lat_total)) / (lat_total * lon_total)
    weighted = (legendre * weights[None, None, :]).astype(jnp.bfloat16)
    legendre = (legendre * factor[None, :, None]).astype(jnp.bfloat16)

    live = jnp.arange(S, dtype=jnp.int32)[None, :] < counts[:, None]
    lanes = taps // tap_span * REACH + taps % tap_span
    matches = (lanes[:, :, None] == jnp.arange(LANES, dtype=jnp.int32)) & live[:, :, None]
    base = jnp.einsum(
        "isq,isk->ikq", matches.astype(jnp.float32), disco_kernel[0], precision=exact_prec
    )

    above, below = halo(normed, "lat", 0, 1, False)
    extended = jnp.concatenate([above, normed, below], axis=0)
    west, east = halo(extended, "lon", 1, R, True)
    blocks = -(-lon_cols // WIDTH)
    spare = blocks * WIDTH - lon_cols
    extended = jnp.concatenate(
        [west, extended, east, jnp.zeros((lat_rows + 2, spare, channels), jnp.bfloat16)], axis=1
    )
    disco = jnp.transpose(disco_update(extended, base, disco_mix[0], lon_cols), (1, 0, 2))

    spectral = []
    for n in range(CUTS):
        gain = filter_gain[0, :, n * cut : (n + 1) * cut]
        spectrum = jnp.einsum(
            "mp,ipc->imc", waves, whole_rows[n], preferred_element_type=jnp.float32
        ).astype(jnp.bfloat16)
        owned = lax.all_to_all(spectrum, ("lat", "lon"), split_axis=1, concat_axis=0, tiled=True)
        owned = owned.reshape(lat_total, 2, modes_own, cut)
        coefficient = jnp.einsum(
            "lmj,jrmc->mlrc", weighted, owned, preferred_element_type=jnp.float32
        )
        scaled = (coefficient * gain[None, :, None, :]).astype(jnp.bfloat16)
        filtered = jnp.einsum(
            "lmj,mlrc->mjrc", legendre, scaled, preferred_element_type=jnp.float32
        ).astype(jnp.bfloat16)
        filtered = jnp.transpose(filtered, (1, 2, 0, 3)).reshape(lat_total, 2 * modes_own, cut)
        returned = lax.all_to_all(
            filtered, ("lat", "lon"), split_axis=0, concat_axis=1, tiled=True
        )
        restored = jnp.einsum(
            "mp,imc->ipc", waves, returned, preferred_element_type=jnp.float32
        ).astype(jnp.bfloat16)
        restored = lax.all_to_all(restored, "lon", split_axis=1, concat_axis=0, tiled=True)
        spectral.append(jnp.transpose(restored, (1, 0, 2)))
    result = mlp_update(
        jnp.transpose(state, (1, 0, 2)), disco, spectral, norm_gain[0, 1:2], mlp_in[0], mlp_out[0]
    )
    return jnp.transpose(result, (1, 0, 2))


def solution(mesh):
    in_specs = (
        P(("grp", "lat"), "lon", None),
        P(),
        P(None, "lat", None, None),
        P("lat", None),
        P("lat"),
        P(),
        P(),
        P(),
        P(),
    )
    out_specs = P(("grp", "lat"), "lon", None)
    return jax.shard_map(local, mesh=mesh, in_specs=in_specs, out_specs=out_specs, check_vma=False)
```

```python
import math

import jax
import jax.numpy as jnp
from jax import lax
from jax.experimental import pallas as pl
from jax.experimental.pallas import tpu as pltpu
from jax.sharding import PartitionSpec as P

M = 256
L = 256
K = 8
R = 8
S = 24
WIDTH = 64
REACH = WIDTH + 2 * R
LANES = 256
STEP = 30

exact_prec = lax.Precision.HIGHEST


def halo(cells, axis, dim, width, closed):
    count = lax.axis_size(axis)
    ends = count if closed else count - 1
    head = lax.slice_in_dim(cells, 0, width, axis=dim)
    tail = lax.slice_in_dim(cells, cells.shape[dim] - width, cells.shape[dim], axis=dim)
    before = lax.ppermute(tail, axis, [(i, (i + 1) % count) for i in range(ends)])
    after = lax.ppermute(head, axis, [((i + 1) % count, i) for i in range(ends)])
    return before, after


def layer_norm(values, gain):
    center = values - jnp.mean(values, axis=-1, keepdims=True)
    spread = jnp.mean(center * center, axis=-1, keepdims=True)
    return center * lax.rsqrt(spread + 1e-05) * gain


def colatitudes(lat_count):
    row_ids = jnp.arange(lat_count).astype(jnp.float32)
    return math.pi * (row_ids + 0.5) / lat_count


def legendre_kernel(orders_ref, cosine_ref, diagonal_ref, out_ref):
    orders = orders_ref[...]
    cosine = cosine_ref[...]
    diagonal = diagonal_ref[...]
    ord_sq = orders * orders
    second_coef = cosine * jnp.sqrt(2.0 * orders + 3.0)

    def advance(step, carry):
        latest, earlier = carry
        degree = step.astype(jnp.float32)
        deg_sq = degree * degree
        upper_coef = jnp.sqrt((4.0 * deg_sq - 1.0) / jnp.maximum(deg_sq - ord_sq, 1.0))
        previous = degree - 1.0
        lower_coef = jnp.sqrt(
            jnp.maximum(previous * previous - ord_sq, 0.0)
            / jnp.maximum(4.0 * previous * previous - 1.0, 1.0)
        )
        recurred = upper_coef * (cosine * latest - lower_coef * earlier)
        current = jnp.where(
            degree < orders,
            0.0,
            jnp.where(
                degree == orders,
                diagonal,
                jnp.where(degree == orders + 1.0, second_coef * latest, recurred),
            ),
        )
        out_ref[step] = current
        return current, latest

    blank = diagonal * 0.0
    lax.fori_loop(0, out_ref.shape[0], advance, (blank, blank), unroll=8)


def legendre_table(mode_ids, lat_count, degrees):
    colatitude = colatitudes(lat_count)
    cosine = jnp.cos(colatitude)[None, :]
    sine_val = jnp.sin(colatitude)[None, :]
    orders = mode_ids.astype(jnp.float32)[:, None]
    factor_ids = jnp.arange(1, degrees + 1).astype(jnp.float32)[None, :]
    log_terms = jnp.where(
        factor_ids <= orders, 0.5 * jnp.log((2.0 * factor_ids - 1.0) / (2.0 * factor_ids)), 0.0
    )
    log_start = 0.5 * jnp.log((2.0 * orders + 1.0) / (4.0 * math.pi)) + jnp.sum(
        log_terms, axis=1, keepdims=True
    )
    diagonal = jnp.exp(log_start + orders * jnp.log(sine_val))
    shape = diagonal.shape
    return pl.pallas_call(
        legendre_kernel,
        out_shape=jax.ShapeDtypeStruct((degrees,) + shape, jnp.float32),
        compiler_params=pltpu.CompilerParams(vmem_limit_bytes=48 * 2**20),
        cost_estimate=pl.CostEstimate(
            flops=40 * degrees * 1024, bytes_accessed=4 * degrees * 2048, transcendentals=0
        ),
        name="legendre",
    )(jnp.broadcast_to(orders, shape), jnp.broadcast_to(cosine, shape), diagonal)


def disco_body(above_ref, here_ref, below_ref, base_ref, mix_ref, out_ref, band_ref):
    cols = out_ref.shape[1]
    for k in range(K):
        row = jnp.broadcast_to(base_ref[0, k : k + 1, :], (WIDTH, LANES))
        band = pltpu.roll(row, 0, 1, stride=1, stride_axis=0)
        band_ref[k * WIDTH : (k + 1) * WIDTH, :] = band.astype(jnp.bfloat16)
    band = band_ref[:, : 3 * REACH]
    pieces = []
    for start in range(0, cols, WIDTH):
        window = jnp.concatenate(
            [ref[0, start : start + REACH, :] for ref in (above_ref, here_ref, below_ref)], axis=0
        )
        conv = jnp.dot(band, window, preferred_element_type=jnp.float32).astype(jnp.bfloat16)
        pieces.append(
            jnp.concatenate([conv[k * WIDTH : (k + 1) * WIDTH] for k in range(K)], axis=1)
        )
    mixed = jnp.dot(
        jnp.concatenate(pieces, axis=0), mix_ref[...], preferred_element_type=jnp.float32
    )
    out_ref[0] = mixed[:cols]


def disco_update(extended, base, mix, cols):
    rows = base.shape[0]
    width, channels = extended.shape[1:]

    def ext_spec(offset):
        return pl.BlockSpec((1, width, channels), lambda i: (i + offset, 0, 0))

    cell = pl.BlockSpec((1, cols, channels), lambda i: (i, 0, 0))
    return pl.pallas_call(
        disco_body,
        grid=(rows,),
        in_specs=[
            ext_spec(0),
            ext_spec(1),
            ext_spec(2),
            pl.BlockSpec((1, K, LANES), lambda i: (i, 0, 0)),
            pl.BlockSpec(mix.shape, lambda i: (0, 0)),
        ],
        out_specs=cell,
        out_shape=jax.ShapeDtypeStruct((rows, cols, channels), jnp.float32),
        scratch_shapes=[pltpu.VMEM((K * WIDTH, LANES), jnp.bfloat16)],
        compiler_params=pltpu.CompilerParams(vmem_limit_bytes=48 * 2**20),
        cost_estimate=pl.CostEstimate(
            flops=2 * rows * cols * K * channels * 512, bytes_accessed=12 * 2**20, transcendentals=0
        ),
        name="disco",
    )(extended, extended, extended, base, mix)


def norm_body(state_ref, gain_ref, out_ref):
    out_ref[...] = layer_norm(state_ref[...], gain_ref[...][None]).astype(jnp.bfloat16)


def norm_update(state, gain):
    cols, rows, channels = state.shape
    step = max(size for size in range(1, STEP + 1) if cols % size == 0)
    cell = pl.BlockSpec((step, rows, channels), lambda i: (i, 0, 0))
    return pl.pallas_call(
        norm_body,
        grid=(cols // step,),
        in_specs=[cell, pl.BlockSpec(gain.shape, lambda i: (0, 0))],
        out_specs=cell,
        out_shape=jax.ShapeDtypeStruct(state.shape, jnp.bfloat16),
        compiler_params=pltpu.CompilerParams(vmem_limit_bytes=48 * 2**20),
        name="norm",
    )(state, gain)


def mlp_body(state_ref, disco_ref, *refs):
    *spectral_refs, gain_ref, in_ref, out_mat_ref, out_ref = refs
    cells = state_ref.shape[0] * state_ref.shape[1]
    channels = state_ref.shape[2]
    spectral = jnp.concatenate([ref[...].astype(jnp.float32) for ref in spectral_refs], axis=2)
    state = (state_ref[...] + disco_ref[...] + spectral).reshape(cells, channels)
    normed = layer_norm(state, gain_ref[...]).astype(jnp.bfloat16)
    hidden = jax.nn.gelu(jnp.dot(normed, in_ref[...], preferred_element_type=jnp.float32))
    state = state + jnp.dot(
        hidden.astype(jnp.bfloat16), out_mat_ref[...], preferred_element_type=jnp.float32
    )
    out_ref[...] = state.reshape(out_ref.shape)


def mlp_update(state, disco, spectral, gain, mat_in, mat_out):
    cols, rows, channels = state.shape
    step = max(size for size in range(1, STEP + 1) if cols % size == 0)
    cell = pl.BlockSpec((step, rows, channels), lambda i: (i, 0, 0))
    return pl.pallas_call(
        mlp_body,
        grid=(cols // step,),
        in_specs=[cell, cell]
        + [pl.BlockSpec((step, rows, part.shape[2]), lambda i: (i, 0, 0)) for part in spectral]
        + [pl.BlockSpec(mat.shape, lambda i: (0, 0)) for mat in (gain, mat_in, mat_out)],
        out_specs=cell,
        out_shape=jax.ShapeDtypeStruct(state.shape, jnp.float32),
        compiler_params=pltpu.CompilerParams(vmem_limit_bytes=48 * 2**20),
        name="mlp",
    )(state, disco, *spectral, gain, mat_in, mat_out)


def local(state, norm_gain, disco_kernel, taps, counts, disco_mix, filter_gain, mlp_in, mlp_out):
    lat_rows, lon_cols, channels = state.shape
    lon_parts = lax.axis_size("lon")
    lat_parts = lax.axis_size("lat")
    parts = lon_parts * lat_parts
    lon_total = lon_cols * lon_parts
    lat_total = lat_rows * lat_parts
    rank = lax.axis_index("lat") * lon_parts + lax.axis_index("lon")
    modes_own = M // parts
    tap_span = 2 * R + 1

    share = lat_rows // lon_parts
    turned = jnp.transpose(state, (1, 0, 2))
    normed = norm_update(turned, norm_gain[0, 0:1])

    slot_ids = jnp.arange(2 * M, dtype=jnp.int32)
    imaginary = slot_ids // modes_own % 2 == 1
    slot_modes = slot_ids // (2 * modes_own) * modes_own + slot_ids % modes_own
    points = jnp.arange(lon_total, dtype=jnp.int32)
    normed, slot_modes = lax.optimization_barrier((normed, slot_modes))
    sent = jnp.transpose(normed.reshape(lon_cols, lon_parts, share, channels), (1, 0, 2, 3))
    whole_rows = lax.all_to_all(sent, "lon", split_axis=0, concat_axis=0, tiled=True)
    whole_rows = whole_rows.reshape(lon_total, share, channels)
    normed = jnp.transpose(normed, (1, 0, 2))
    above, below = halo(normed, "lat", 0, 1, False)
    whole_rows, above, below = lax.optimization_barrier((whole_rows, above, below))
    quarter = jnp.where(imaginary, lon_total // 4, 0)
    steps = (slot_modes[:, None] * points[None, :] + quarter[:, None]) % lon_total
    waves = jnp.cos(steps.astype(jnp.float32) * (2.0 * math.pi / lon_total)).astype(jnp.bfloat16)
    waves = lax.optimization_barrier(waves)

    own_modes = rank * modes_own + jnp.arange(modes_own, dtype=jnp.int32)
    factor = jnp.where(own_modes == 0, 1.0, 2.0).astype(jnp.float32)
    legendre = legendre_table(own_modes, lat_total, L)
    weights = math.pi * jnp.sin(colatitudes(lat_total)) / (lat_total * lon_total)
    weighted = (legendre * weights[None, None, :]).astype(jnp.bfloat16)
    legendre = (legendre * factor[None, :, None]).astype(jnp.bfloat16)

    live = jnp.arange(S, dtype=jnp.int32)[None, :] < counts[:, None]
    lanes = taps // tap_span * REACH + taps % tap_span
    matches = (lanes[:, :, None] == jnp.arange(LANES, dtype=jnp.int32)) & live[:, :, None]
    base = jnp.einsum(
        "isq,isk->ikq", matches.astype(jnp.float32), disco_kernel[0], precision=exact_prec
    )

    extended = jnp.concatenate([above, normed, below], axis=0)
    west, east = halo(extended, "lon", 1, R, True)
    blocks = -(-lon_cols // WIDTH)
    spare = blocks * WIDTH - lon_cols

    spectrum = jnp.einsum(
        "mp,pic->mic", waves, whole_rows, preferred_element_type=jnp.float32
    ).astype(jnp.bfloat16)
    owned = lax.all_to_all(spectrum, ("lat", "lon"), split_axis=0, concat_axis=0, tiled=True)
    owned, west, east = lax.optimization_barrier((owned, west, east))
    extended = jnp.concatenate(
        [west, extended, east, jnp.zeros((lat_rows + 2, spare, channels), jnp.bfloat16)], axis=1
    )
    disco = jnp.transpose(disco_update(extended, base, disco_mix[0], lon_cols), (1, 0, 2))
    owned = owned.reshape(parts, 2, modes_own, share, channels)
    owned = jnp.transpose(owned, (2, 0, 3, 1, 4)).reshape(modes_own, lat_total, 2, channels)
    coefficient = jnp.einsum(
        "lmj,mjrc->mlrc", weighted, owned, preferred_element_type=jnp.float32
    )
    scaled = (coefficient * filter_gain[0][None, :, None, :]).astype(jnp.bfloat16)
    filtered = jnp.einsum(
        "lmj,mlrc->mjrc", legendre, scaled, preferred_element_type=jnp.float32
    ).astype(jnp.bfloat16)
    filtered = jnp.transpose(filtered, (1, 2, 0, 3)).reshape(lat_total, 2 * modes_own, channels)
    returned = lax.all_to_all(filtered, ("lat", "lon"), split_axis=0, concat_axis=1, tiled=True)
    restored = jnp.einsum(
        "mp,imc->pic", waves, returned, preferred_element_type=jnp.float32
    ).astype(jnp.bfloat16)
    restored = restored.reshape(lon_parts, lon_cols, share, channels)
    spectral = lax.all_to_all(restored, "lon", split_axis=0, concat_axis=0, tiled=True)
    spectral = jnp.transpose(spectral, (1, 0, 2, 3)).reshape(lon_cols, lat_rows, channels)
    result = mlp_update(turned, disco, [spectral], norm_gain[0, 1:2], mlp_in[0], mlp_out[0])
    return jnp.transpose(result, (1, 0, 2))


def solution(mesh):
    in_specs = (
        P(("grp", "lat"), "lon", None),
        P(),
        P(None, "lat", None, None),
        P("lat", None),
        P("lat"),
        P(),
        P(),
        P(),
        P(),
    )
    out_specs = P(("grp", "lat"), "lon", None)
    return jax.shard_map(local, mesh=mesh, in_specs=in_specs, out_specs=out_specs, check_vma=False)
```

```python
import math

import jax
import jax.numpy as jnp
from jax import lax
from jax.experimental import pallas as pl
from jax.experimental.pallas import tpu as pltpu
from jax.sharding import PartitionSpec as P

M = 256
L = 256
K = 8
R = 8
S = 24
WIDTH = 64
REACH = WIDTH + 2 * R
LANES = 256
STEP = 30

exact_prec = lax.Precision.HIGHEST


def halo(cells, axis, dim, width, closed):
    count = lax.axis_size(axis)
    ends = count if closed else count - 1
    head = lax.slice_in_dim(cells, 0, width, axis=dim)
    tail = lax.slice_in_dim(cells, cells.shape[dim] - width, cells.shape[dim], axis=dim)
    before = lax.ppermute(tail, axis, [(i, (i + 1) % count) for i in range(ends)])
    after = lax.ppermute(head, axis, [((i + 1) % count, i) for i in range(ends)])
    return before, after


def layer_norm(values, gain):
    center = values - jnp.mean(values, axis=-1, keepdims=True)
    spread = jnp.mean(center * center, axis=-1, keepdims=True)
    return center * lax.rsqrt(spread + 1e-05) * gain


def colatitudes(lat_count):
    row_ids = jnp.arange(lat_count).astype(jnp.float32)
    return math.pi * (row_ids + 0.5) / lat_count


def legendre_kernel(orders_ref, cosine_ref, diagonal_ref, out_ref):
    orders = orders_ref[...]
    cosine = cosine_ref[...]
    diagonal = diagonal_ref[...]
    ord_sq = orders * orders
    second_coef = cosine * jnp.sqrt(2.0 * orders + 3.0)

    def advance(step, carry):
        latest, earlier = carry
        degree = step.astype(jnp.float32)
        deg_sq = degree * degree
        upper_coef = jnp.sqrt((4.0 * deg_sq - 1.0) / jnp.maximum(deg_sq - ord_sq, 1.0))
        previous = degree - 1.0
        lower_coef = jnp.sqrt(
            jnp.maximum(previous * previous - ord_sq, 0.0)
            / jnp.maximum(4.0 * previous * previous - 1.0, 1.0)
        )
        recurred = upper_coef * (cosine * latest - lower_coef * earlier)
        current = jnp.where(
            degree < orders,
            0.0,
            jnp.where(
                degree == orders,
                diagonal,
                jnp.where(degree == orders + 1.0, second_coef * latest, recurred),
            ),
        )
        out_ref[step] = current
        return current, latest

    blank = diagonal * 0.0
    lax.fori_loop(0, out_ref.shape[0], advance, (blank, blank), unroll=8)


def legendre_table(mode_ids, lat_count, degrees):
    colatitude = colatitudes(lat_count)
    cosine = jnp.cos(colatitude)[None, :]
    sine_val = jnp.sin(colatitude)[None, :]
    orders = mode_ids.astype(jnp.float32)[:, None]
    factor_ids = jnp.arange(1, degrees + 1).astype(jnp.float32)[None, :]
    log_terms = jnp.where(
        factor_ids <= orders, 0.5 * jnp.log((2.0 * factor_ids - 1.0) / (2.0 * factor_ids)), 0.0
    )
    log_start = 0.5 * jnp.log((2.0 * orders + 1.0) / (4.0 * math.pi)) + jnp.sum(
        log_terms, axis=1, keepdims=True
    )
    diagonal = jnp.exp(log_start + orders * jnp.log(sine_val))
    shape = diagonal.shape
    return pl.pallas_call(
        legendre_kernel,
        out_shape=jax.ShapeDtypeStruct((degrees,) + shape, jnp.float32),
        compiler_params=pltpu.CompilerParams(vmem_limit_bytes=48 * 2**20),
        cost_estimate=pl.CostEstimate(
            flops=40 * degrees * 1024, bytes_accessed=4 * degrees * 2048, transcendentals=0
        ),
        name="legendre",
    )(jnp.broadcast_to(orders, shape), jnp.broadcast_to(cosine, shape), diagonal)


def disco_body(above_ref, here_ref, below_ref, base_ref, mix_ref, out_ref, band_ref):
    cols = out_ref.shape[1]
    for k in range(K):
        row = jnp.broadcast_to(base_ref[0, k : k + 1, :], (WIDTH, LANES))
        band = pltpu.roll(row, 0, 1, stride=1, stride_axis=0)
        band_ref[k * WIDTH : (k + 1) * WIDTH, :] = band.astype(jnp.bfloat16)
    band = band_ref[:, : 3 * REACH]
    pieces = []
    for start in range(0, cols, WIDTH):
        window = jnp.concatenate(
            [ref[0, start : start + REACH, :] for ref in (above_ref, here_ref, below_ref)], axis=0
        )
        conv = jnp.dot(band, window, preferred_element_type=jnp.float32).astype(jnp.bfloat16)
        pieces.append(
            jnp.concatenate([conv[k * WIDTH : (k + 1) * WIDTH] for k in range(K)], axis=1)
        )
    mixed = jnp.dot(
        jnp.concatenate(pieces, axis=0), mix_ref[...], preferred_element_type=jnp.float32
    )
    out_ref[0] = mixed[:cols]


def disco_update(extended, base, mix, cols):
    rows = base.shape[0]
    width, channels = extended.shape[1:]

    def ext_spec(offset):
        return pl.BlockSpec((1, width, channels), lambda i: (i + offset, 0, 0))

    cell = pl.BlockSpec((1, cols, channels), lambda i: (i, 0, 0))
    return pl.pallas_call(
        disco_body,
        grid=(rows,),
        in_specs=[
            ext_spec(0),
            ext_spec(1),
            ext_spec(2),
            pl.BlockSpec((1, K, LANES), lambda i: (i, 0, 0)),
            pl.BlockSpec(mix.shape, lambda i: (0, 0)),
        ],
        out_specs=cell,
        out_shape=jax.ShapeDtypeStruct((rows, cols, channels), jnp.float32),
        scratch_shapes=[pltpu.VMEM((K * WIDTH, LANES), jnp.bfloat16)],
        compiler_params=pltpu.CompilerParams(vmem_limit_bytes=48 * 2**20),
        cost_estimate=pl.CostEstimate(
            flops=2 * rows * cols * K * channels * 512, bytes_accessed=12 * 2**20, transcendentals=0
        ),
        name="disco",
    )(extended, extended, extended, base, mix)


def norm_body(state_ref, gain_ref, out_ref):
    out_ref[...] = layer_norm(state_ref[...], gain_ref[...][None]).astype(jnp.bfloat16)


def norm_update(state, gain):
    cols, rows, channels = state.shape
    step = max(size for size in range(1, STEP + 1) if cols % size == 0)
    cell = pl.BlockSpec((step, rows, channels), lambda i: (i, 0, 0))
    return pl.pallas_call(
        norm_body,
        grid=(cols // step,),
        in_specs=[cell, pl.BlockSpec(gain.shape, lambda i: (0, 0))],
        out_specs=cell,
        out_shape=jax.ShapeDtypeStruct(state.shape, jnp.bfloat16),
        compiler_params=pltpu.CompilerParams(vmem_limit_bytes=48 * 2**20),
        name="norm",
    )(state, gain)


def mlp_body(state_ref, disco_ref, spectral_ref, gain_ref, in_ref, out_mat_ref, out_ref):
    cells = state_ref.shape[0] * state_ref.shape[1]
    channels = state_ref.shape[2]
    spectral = jnp.concatenate(
        [spectral_ref[n].astype(jnp.float32) for n in range(spectral_ref.shape[0])], axis=1
    )
    state = (state_ref[...] + disco_ref[...] + spectral).reshape(cells, channels)
    normed = layer_norm(state, gain_ref[...]).astype(jnp.bfloat16)
    hidden = jax.nn.gelu(jnp.dot(normed, in_ref[...], preferred_element_type=jnp.float32))
    state = state + jnp.dot(
        hidden.astype(jnp.bfloat16), out_mat_ref[...], preferred_element_type=jnp.float32
    )
    out_ref[...] = state.reshape(out_ref.shape)


def mlp_update(state, disco, spectral, gain, mat_in, mat_out):
    cols, rows, channels = state.shape
    lon_parts, share = spectral.shape[0], spectral.shape[2]
    step = max(size for size in range(1, STEP + 1) if cols % size == 0)
    cell = pl.BlockSpec((step, rows, channels), lambda i: (i, 0, 0))
    return pl.pallas_call(
        mlp_body,
        grid=(cols // step,),
        in_specs=[cell, cell]
        + [pl.BlockSpec((lon_parts, step, share, channels), lambda i: (0, i, 0, 0))]
        + [pl.BlockSpec(mat.shape, lambda i: (0, 0)) for mat in (gain, mat_in, mat_out)],
        out_specs=cell,
        out_shape=jax.ShapeDtypeStruct(state.shape, jnp.float32),
        compiler_params=pltpu.CompilerParams(vmem_limit_bytes=48 * 2**20),
        name="mlp",
    )(state, disco, spectral, gain, mat_in, mat_out)


def local(state, norm_gain, disco_kernel, taps, counts, disco_mix, filter_gain, mlp_in, mlp_out):
    lat_rows, lon_cols, channels = state.shape
    lon_parts = lax.axis_size("lon")
    lat_parts = lax.axis_size("lat")
    parts = lon_parts * lat_parts
    lon_total = lon_cols * lon_parts
    lat_total = lat_rows * lat_parts
    rank = lax.axis_index("lat") * lon_parts + lax.axis_index("lon")
    modes_own = M // parts
    tap_span = 2 * R + 1

    share = lat_rows // lon_parts
    turned = jnp.transpose(state, (1, 0, 2))
    normed = norm_update(turned, norm_gain[0, 0:1])

    slot_ids = jnp.arange(2 * M, dtype=jnp.int32)
    imaginary = slot_ids // modes_own % 2 == 1
    slot_modes = slot_ids // (2 * modes_own) * modes_own + slot_ids % modes_own
    points = jnp.arange(lon_total, dtype=jnp.int32)
    normed, slot_modes = lax.optimization_barrier((normed, slot_modes))
    sent = jnp.transpose(normed.reshape(lon_cols, lon_parts, share, channels), (1, 0, 2, 3))
    whole_rows = lax.all_to_all(sent, "lon", split_axis=0, concat_axis=0, tiled=True)
    whole_rows = whole_rows.reshape(lon_total, share, channels)
    normed = jnp.transpose(normed, (1, 0, 2))
    above, below = halo(normed, "lat", 0, 1, False)
    whole_rows, above, below = lax.optimization_barrier((whole_rows, above, below))
    quarter = jnp.where(imaginary, lon_total // 4, 0)
    steps = (slot_modes[:, None] * points[None, :] + quarter[:, None]) % lon_total
    waves = jnp.cos(steps.astype(jnp.float32) * (2.0 * math.pi / lon_total)).astype(jnp.bfloat16)
    waves = lax.optimization_barrier(waves)

    own_modes = rank * modes_own + jnp.arange(modes_own, dtype=jnp.int32)
    factor = jnp.where(own_modes == 0, 1.0, 2.0).astype(jnp.float32)
    legendre = legendre_table(own_modes, lat_total, L)
    weights = math.pi * jnp.sin(colatitudes(lat_total)) / (lat_total * lon_total)
    weighted = (legendre * weights[None, None, :]).astype(jnp.bfloat16)
    legendre = (legendre * factor[None, :, None]).astype(jnp.bfloat16)

    live = jnp.arange(S, dtype=jnp.int32)[None, :] < counts[:, None]
    lanes = taps // tap_span * REACH + taps % tap_span
    matches = (lanes[:, :, None] == jnp.arange(LANES, dtype=jnp.int32)) & live[:, :, None]
    base = jnp.einsum(
        "isq,isk->ikq", matches.astype(jnp.float32), disco_kernel[0], precision=exact_prec
    )

    extended = jnp.concatenate([above, normed, below], axis=0)
    west, east = halo(extended, "lon", 1, R, True)
    blocks = -(-lon_cols // WIDTH)
    spare = blocks * WIDTH - lon_cols

    spectrum = jnp.einsum(
        "mp,pic->mic", waves, whole_rows, preferred_element_type=jnp.float32
    ).astype(jnp.bfloat16)
    owned = lax.all_to_all(spectrum, ("lat", "lon"), split_axis=0, concat_axis=0, tiled=True)
    owned, west, east = lax.optimization_barrier((owned, west, east))
    extended = jnp.concatenate(
        [west, extended, east, jnp.zeros((lat_rows + 2, spare, channels), jnp.bfloat16)], axis=1
    )
    disco = jnp.transpose(disco_update(extended, base, disco_mix[0], lon_cols), (1, 0, 2))
    owned = owned.reshape(parts, 2, modes_own, share, channels)
    owned = jnp.transpose(owned, (2, 0, 3, 1, 4)).reshape(modes_own, lat_total, 2, channels)
    coefficient = jnp.einsum(
        "lmj,mjrc->mlrc", weighted, owned, preferred_element_type=jnp.float32
    )
    scaled = (coefficient * filter_gain[0][None, :, None, :]).astype(jnp.bfloat16)
    filtered = jnp.einsum(
        "lmj,mlrc->mjrc", legendre, scaled, preferred_element_type=jnp.float32
    ).astype(jnp.bfloat16)
    filtered = jnp.transpose(filtered, (1, 2, 0, 3)).reshape(lat_total, 2 * modes_own, channels)
    returned = lax.all_to_all(filtered, ("lat", "lon"), split_axis=0, concat_axis=1, tiled=True)
    restored = jnp.einsum(
        "mp,imc->pic", waves, returned, preferred_element_type=jnp.float32
    ).astype(jnp.bfloat16)
    restored = restored.reshape(lon_parts, lon_cols, share, channels)
    spectral = lax.all_to_all(restored, "lon", split_axis=0, concat_axis=0, tiled=True)
    result = mlp_update(turned, disco, spectral, norm_gain[0, 1:2], mlp_in[0], mlp_out[0])
    return jnp.transpose(result, (1, 0, 2))


def solution(mesh):
    in_specs = (
        P(("grp", "lat"), "lon", None),
        P(),
        P(None, "lat", None, None),
        P("lat", None),
        P("lat"),
        P(),
        P(),
        P(),
        P(),
    )
    out_specs = P(("grp", "lat"), "lon", None)
    return jax.shard_map(local, mesh=mesh, in_specs=in_specs, out_specs=out_specs, check_vma=False)
```

```python
import math

import jax
import jax.numpy as jnp
from jax import lax
from jax.experimental import pallas as pl
from jax.experimental.pallas import tpu as pltpu
from jax.sharding import PartitionSpec as P

M = 256
L = 256
K = 8
R = 8
S = 24
WIDTH = 64
REACH = WIDTH + 2 * R
LANES = 256
STEP = 30

exact_prec = lax.Precision.HIGHEST


def halo(cells, axis, dim, width, closed):
    count = lax.axis_size(axis)
    ends = count if closed else count - 1
    head = lax.slice_in_dim(cells, 0, width, axis=dim)
    tail = lax.slice_in_dim(cells, cells.shape[dim] - width, cells.shape[dim], axis=dim)
    before = lax.ppermute(tail, axis, [(i, (i + 1) % count) for i in range(ends)])
    after = lax.ppermute(head, axis, [((i + 1) % count, i) for i in range(ends)])
    return before, after


def layer_norm(values, gain):
    center = values - jnp.mean(values, axis=-1, keepdims=True)
    spread = jnp.mean(center * center, axis=-1, keepdims=True)
    return center * lax.rsqrt(spread + 1e-05) * gain


def colatitudes(lat_count):
    row_ids = jnp.arange(lat_count).astype(jnp.float32)
    return math.pi * (row_ids + 0.5) / lat_count


def legendre_kernel(orders_ref, cosine_ref, diagonal_ref, out_ref):
    orders = orders_ref[...]
    cosine = cosine_ref[...]
    diagonal = diagonal_ref[...]
    ord_sq = orders * orders
    second_coef = cosine * jnp.sqrt(2.0 * orders + 3.0)

    def advance(step, carry):
        latest, earlier = carry
        degree = step.astype(jnp.float32)
        deg_sq = degree * degree
        upper_coef = jnp.sqrt((4.0 * deg_sq - 1.0) / jnp.maximum(deg_sq - ord_sq, 1.0))
        previous = degree - 1.0
        lower_coef = jnp.sqrt(
            jnp.maximum(previous * previous - ord_sq, 0.0)
            / jnp.maximum(4.0 * previous * previous - 1.0, 1.0)
        )
        recurred = upper_coef * (cosine * latest - lower_coef * earlier)
        current = jnp.where(
            degree < orders,
            0.0,
            jnp.where(
                degree == orders,
                diagonal,
                jnp.where(degree == orders + 1.0, second_coef * latest, recurred),
            ),
        )
        out_ref[step] = current
        return current, latest

    blank = diagonal * 0.0
    lax.fori_loop(0, out_ref.shape[0], advance, (blank, blank), unroll=8)


def legendre_table(mode_ids, lat_count, degrees):
    colatitude = colatitudes(lat_count)
    cosine = jnp.cos(colatitude)[None, :]
    sine_val = jnp.sin(colatitude)[None, :]
    orders = mode_ids.astype(jnp.float32)[:, None]
    factor_ids = jnp.arange(1, degrees + 1).astype(jnp.float32)[None, :]
    log_terms = jnp.where(
        factor_ids <= orders, 0.5 * jnp.log((2.0 * factor_ids - 1.0) / (2.0 * factor_ids)), 0.0
    )
    log_start = 0.5 * jnp.log((2.0 * orders + 1.0) / (4.0 * math.pi)) + jnp.sum(
        log_terms, axis=1, keepdims=True
    )
    diagonal = jnp.exp(log_start + orders * jnp.log(sine_val))
    shape = diagonal.shape
    return pl.pallas_call(
        legendre_kernel,
        out_shape=jax.ShapeDtypeStruct((degrees,) + shape, jnp.float32),
        compiler_params=pltpu.CompilerParams(vmem_limit_bytes=48 * 2**20),
        cost_estimate=pl.CostEstimate(
            flops=40 * degrees * 1024, bytes_accessed=4 * degrees * 2048, transcendentals=0
        ),
        name="legendre",
    )(jnp.broadcast_to(orders, shape), jnp.broadcast_to(cosine, shape), diagonal)


def disco_body(above_ref, here_ref, below_ref, base_ref, mix_ref, out_ref, band_ref):
    cols = out_ref.shape[1]
    for k in range(K):
        row = jnp.broadcast_to(base_ref[0, k : k + 1, :], (WIDTH, LANES))
        band = pltpu.roll(row, 0, 1, stride=1, stride_axis=0)
        band_ref[k * WIDTH : (k + 1) * WIDTH, :] = band.astype(jnp.bfloat16)
    band = band_ref[:, : 3 * REACH]
    pieces = []
    for start in range(0, cols, WIDTH):
        window = jnp.concatenate(
            [ref[0, start : start + REACH, :] for ref in (above_ref, here_ref, below_ref)], axis=0
        )
        conv = jnp.dot(band, window, preferred_element_type=jnp.float32).astype(jnp.bfloat16)
        pieces.append(
            jnp.concatenate([conv[k * WIDTH : (k + 1) * WIDTH] for k in range(K)], axis=1)
        )
    mixed = jnp.dot(
        jnp.concatenate(pieces, axis=0), mix_ref[...], preferred_element_type=jnp.float32
    )
    out_ref[0] = mixed[:cols]


def disco_update(extended, base, mix, cols):
    rows = base.shape[0]
    width, channels = extended.shape[1:]

    def ext_spec(offset):
        return pl.BlockSpec((1, width, channels), lambda i: (i + offset, 0, 0))

    cell = pl.BlockSpec((1, cols, channels), lambda i: (i, 0, 0))
    return pl.pallas_call(
        disco_body,
        grid=(rows,),
        in_specs=[
            ext_spec(0),
            ext_spec(1),
            ext_spec(2),
            pl.BlockSpec((1, K, LANES), lambda i: (i, 0, 0)),
            pl.BlockSpec(mix.shape, lambda i: (0, 0)),
        ],
        out_specs=cell,
        out_shape=jax.ShapeDtypeStruct((rows, cols, channels), jnp.float32),
        scratch_shapes=[pltpu.VMEM((K * WIDTH, LANES), jnp.bfloat16)],
        compiler_params=pltpu.CompilerParams(vmem_limit_bytes=48 * 2**20),
        cost_estimate=pl.CostEstimate(
            flops=2 * rows * cols * K * channels * 512, bytes_accessed=12 * 2**20, transcendentals=0
        ),
        name="disco",
    )(extended, extended, extended, base, mix)


def norm_body(state_ref, gain_ref, out_ref):
    out_ref[...] = layer_norm(state_ref[...], gain_ref[...][None]).astype(jnp.bfloat16)


def norm_update(state, gain):
    cols, rows, channels = state.shape
    step = max(size for size in range(1, STEP + 1) if cols % size == 0)
    cell = pl.BlockSpec((step, rows, channels), lambda i: (i, 0, 0))
    return pl.pallas_call(
        norm_body,
        grid=(cols // step,),
        in_specs=[cell, pl.BlockSpec(gain.shape, lambda i: (0, 0))],
        out_specs=cell,
        out_shape=jax.ShapeDtypeStruct(state.shape, jnp.bfloat16),
        compiler_params=pltpu.CompilerParams(vmem_limit_bytes=48 * 2**20),
        name="norm",
    )(state, gain)


def mlp_body(state_ref, disco_ref, spectral_ref, gain_ref, in_ref, out_mat_ref, out_ref):
    cells = state_ref.shape[0] * state_ref.shape[1]
    channels = state_ref.shape[2]
    spectral = jnp.concatenate(
        [spectral_ref[n].astype(jnp.float32) for n in range(spectral_ref.shape[0])], axis=1
    )
    state = (state_ref[...] + disco_ref[...] + spectral).reshape(cells, channels)
    normed = layer_norm(state, gain_ref[...]).astype(jnp.bfloat16)
    hidden = jax.nn.gelu(jnp.dot(normed, in_ref[...], preferred_element_type=jnp.float32))
    state = state + jnp.dot(
        hidden.astype(jnp.bfloat16), out_mat_ref[...], preferred_element_type=jnp.float32
    )
    out_ref[...] = state.reshape(out_ref.shape)


def mlp_update(state, disco, spectral, gain, mat_in, mat_out):
    cols, rows, channels = state.shape
    lon_parts, share = spectral.shape[0], spectral.shape[2]
    step = max(size for size in range(1, STEP + 1) if cols % size == 0)
    cell = pl.BlockSpec((step, rows, channels), lambda i: (i, 0, 0))
    return pl.pallas_call(
        mlp_body,
        grid=(cols // step,),
        in_specs=[cell, cell]
        + [pl.BlockSpec((lon_parts, step, share, channels), lambda i: (0, i, 0, 0))]
        + [pl.BlockSpec(mat.shape, lambda i: (0, 0)) for mat in (gain, mat_in, mat_out)],
        out_specs=cell,
        out_shape=jax.ShapeDtypeStruct(state.shape, jnp.float32),
        compiler_params=pltpu.CompilerParams(vmem_limit_bytes=48 * 2**20),
        name="mlp",
    )(state, disco, spectral, gain, mat_in, mat_out)


def local(state, norm_gain, disco_kernel, taps, counts, disco_mix, filter_gain, mlp_in, mlp_out):
    lat_rows, lon_cols, channels = state.shape
    lon_parts = lax.axis_size("lon")
    lat_parts = lax.axis_size("lat")
    parts = lon_parts * lat_parts
    lon_total = lon_cols * lon_parts
    lat_total = lat_rows * lat_parts
    rank = lax.axis_index("lat") * lon_parts + lax.axis_index("lon")
    modes_own = M // parts
    tap_span = 2 * R + 1

    share = lat_rows // lon_parts
    turned = jnp.transpose(state, (1, 0, 2))
    normed = norm_update(turned, norm_gain[0, 0:1])

    slot_ids = jnp.arange(2 * M, dtype=jnp.int32)
    imaginary = slot_ids // modes_own % 2 == 1
    slot_modes = slot_ids // (2 * modes_own) * modes_own + slot_ids % modes_own
    points = jnp.arange(lon_total, dtype=jnp.int32)
    normed, slot_modes = lax.optimization_barrier((normed, slot_modes))
    sent = jnp.transpose(normed.reshape(lon_cols, lon_parts, share, channels), (1, 0, 2, 3))
    whole_rows = lax.all_to_all(sent, "lon", split_axis=0, concat_axis=0, tiled=True)
    whole_rows = whole_rows.reshape(lon_total, share, channels)
    normed = jnp.transpose(normed, (1, 0, 2))
    above, below = halo(normed, "lat", 0, 1, False)
    whole_rows, above, below = lax.optimization_barrier((whole_rows, above, below))
    quarter = jnp.where(imaginary, lon_total // 4, 0)
    steps = (slot_modes[:, None] * points[None, :] + quarter[:, None]) % lon_total
    waves = jnp.cos(steps.astype(jnp.float32) * (2.0 * math.pi / lon_total)).astype(jnp.bfloat16)
    waves = lax.optimization_barrier(waves)

    own_modes = rank * modes_own + jnp.arange(modes_own, dtype=jnp.int32)
    factor = jnp.where(own_modes == 0, 1.0, 2.0).astype(jnp.float32)
    legendre = legendre_table(own_modes, lat_total, L)
    weights = math.pi * jnp.sin(colatitudes(lat_total)) / (lat_total * lon_total)
    weighted = (legendre * (factor[:, None] * weights[None, :])[None]).astype(jnp.bfloat16)
    legendre = legendre.astype(jnp.bfloat16)

    live = jnp.arange(S, dtype=jnp.int32)[None, :] < counts[:, None]
    lanes = taps // tap_span * REACH + taps % tap_span
    matches = (lanes[:, :, None] == jnp.arange(LANES, dtype=jnp.int32)) & live[:, :, None]
    base = jnp.einsum(
        "isq,isk->ikq", matches.astype(jnp.float32), disco_kernel[0], precision=exact_prec
    )

    extended = jnp.concatenate([above, normed, below], axis=0)
    west, east = halo(extended, "lon", 1, R, True)
    blocks = -(-lon_cols // WIDTH)
    spare = blocks * WIDTH - lon_cols

    spectrum = jnp.einsum(
        "mp,pic->mic", waves, whole_rows, preferred_element_type=jnp.float32
    ).astype(jnp.bfloat16)
    owned = lax.all_to_all(spectrum, ("lat", "lon"), split_axis=0, concat_axis=0, tiled=True)
    owned, west, east = lax.optimization_barrier((owned, west, east))
    extended = jnp.concatenate(
        [west, extended, east, jnp.zeros((lat_rows + 2, spare, channels), jnp.bfloat16)], axis=1
    )
    disco = jnp.transpose(disco_update(extended, base, disco_mix[0], lon_cols), (1, 0, 2))
    owned = owned.reshape(parts, 2, modes_own, share, channels)
    owned = jnp.transpose(owned, (0, 3, 1, 2, 4)).reshape(lat_total, 2, modes_own, channels)
    coefficient = jnp.einsum(
        "lmj,jrmc->mlrc", weighted, owned, preferred_element_type=jnp.float32
    )
    scaled = (coefficient * filter_gain[0][None, :, None, :]).astype(jnp.bfloat16)
    filtered = jnp.einsum(
        "lmj,mlrc->mjrc", legendre, scaled, preferred_element_type=jnp.float32
    ).astype(jnp.bfloat16)
    filtered = jnp.transpose(filtered, (1, 2, 0, 3)).reshape(lat_total, 2 * modes_own, channels)
    returned = lax.all_to_all(filtered, ("lat", "lon"), split_axis=0, concat_axis=1, tiled=True)
    restored = jnp.einsum(
        "mp,imc->pic", waves, returned, preferred_element_type=jnp.float32
    ).astype(jnp.bfloat16)
    restored = restored.reshape(lon_parts, lon_cols, share, channels)
    spectral = lax.all_to_all(restored, "lon", split_axis=0, concat_axis=0, tiled=True)
    result = mlp_update(turned, disco, spectral, norm_gain[0, 1:2], mlp_in[0], mlp_out[0])
    return jnp.transpose(result, (1, 0, 2))


def solution(mesh):
    in_specs = (
        P(("grp", "lat"), "lon", None),
        P(),
        P(None, "lat", None, None),
        P("lat", None),
        P("lat"),
        P(),
        P(),
        P(),
        P(),
    )
    out_specs = P(("grp", "lat"), "lon", None)
    return jax.shard_map(local, mesh=mesh, in_specs=in_specs, out_specs=out_specs, check_vma=False)
```

```python
import math

import jax
import jax.numpy as jnp
from jax import lax
from jax.experimental import pallas as pl
from jax.experimental.pallas import tpu as pltpu
from jax.sharding import PartitionSpec as P

M = 256
L = 256
K = 8
R = 8
S = 24
WIDTH = 64
REACH = WIDTH + 2 * R
LANES = 256
STEP = 60

exact_prec = lax.Precision.HIGHEST


def halo(cells, axis, dim, width, closed):
    count = lax.axis_size(axis)
    ends = count if closed else count - 1
    head = lax.slice_in_dim(cells, 0, width, axis=dim)
    tail = lax.slice_in_dim(cells, cells.shape[dim] - width, cells.shape[dim], axis=dim)
    before = lax.ppermute(tail, axis, [(i, (i + 1) % count) for i in range(ends)])
    after = lax.ppermute(head, axis, [((i + 1) % count, i) for i in range(ends)])
    return before, after


def layer_norm(values, gain):
    center = values - jnp.mean(values, axis=-1, keepdims=True)
    spread = jnp.mean(center * center, axis=-1, keepdims=True)
    return center * lax.rsqrt(spread + 1e-05) * gain


def colatitudes(lat_count):
    row_ids = jnp.arange(lat_count).astype(jnp.float32)
    return math.pi * (row_ids + 0.5) / lat_count


def legendre_kernel(orders_ref, cosine_ref, diagonal_ref, out_ref):
    orders = orders_ref[...]
    cosine = cosine_ref[...]
    diagonal = diagonal_ref[...]
    ord_sq = orders * orders
    second_coef = cosine * jnp.sqrt(2.0 * orders + 3.0)

    def advance(step, carry):
        latest, earlier = carry
        degree = step.astype(jnp.float32)
        deg_sq = degree * degree
        upper_coef = jnp.sqrt((4.0 * deg_sq - 1.0) / jnp.maximum(deg_sq - ord_sq, 1.0))
        previous = degree - 1.0
        lower_coef = jnp.sqrt(
            jnp.maximum(previous * previous - ord_sq, 0.0)
            / jnp.maximum(4.0 * previous * previous - 1.0, 1.0)
        )
        recurred = upper_coef * (cosine * latest - lower_coef * earlier)
        current = jnp.where(
            degree < orders,
            0.0,
            jnp.where(
                degree == orders,
                diagonal,
                jnp.where(degree == orders + 1.0, second_coef * latest, recurred),
            ),
        )
        out_ref[step] = current
        return current, latest

    blank = diagonal * 0.0
    lax.fori_loop(0, out_ref.shape[0], advance, (blank, blank), unroll=8)


def legendre_table(mode_ids, lat_count, degrees):
    colatitude = colatitudes(lat_count)
    cosine = jnp.cos(colatitude)[None, :]
    sine_val = jnp.sin(colatitude)[None, :]
    orders = mode_ids.astype(jnp.float32)[:, None]
    factor_ids = jnp.arange(1, degrees + 1).astype(jnp.float32)[None, :]
    log_terms = jnp.where(
        factor_ids <= orders, 0.5 * jnp.log((2.0 * factor_ids - 1.0) / (2.0 * factor_ids)), 0.0
    )
    log_start = 0.5 * jnp.log((2.0 * orders + 1.0) / (4.0 * math.pi)) + jnp.sum(
        log_terms, axis=1, keepdims=True
    )
    diagonal = jnp.exp(log_start + orders * jnp.log(sine_val))
    shape = diagonal.shape
    return pl.pallas_call(
        legendre_kernel,
        out_shape=jax.ShapeDtypeStruct((degrees,) + shape, jnp.float32),
        compiler_params=pltpu.CompilerParams(vmem_limit_bytes=48 * 2**20),
        cost_estimate=pl.CostEstimate(
            flops=40 * degrees * 1024, bytes_accessed=4 * degrees * 2048, transcendentals=0
        ),
        name="legendre",
    )(jnp.broadcast_to(orders, shape), jnp.broadcast_to(cosine, shape), diagonal)


def disco_body(above_ref, here_ref, below_ref, base_ref, mix_ref, out_ref, band_ref):
    cols = out_ref.shape[1]
    for k in range(K):
        row = jnp.broadcast_to(base_ref[0, k : k + 1, :], (WIDTH, LANES))
        band = pltpu.roll(row, 0, 1, stride=1, stride_axis=0)
        band_ref[k * WIDTH : (k + 1) * WIDTH, :] = band.astype(jnp.bfloat16)
    band = band_ref[:, : 3 * REACH]
    pieces = []
    for start in range(0, cols, WIDTH):
        window = jnp.concatenate(
            [ref[0, start : start + REACH, :] for ref in (above_ref, here_ref, below_ref)], axis=0
        )
        conv = jnp.dot(band, window, preferred_element_type=jnp.float32).astype(jnp.bfloat16)
        pieces.append(
            jnp.concatenate([conv[k * WIDTH : (k + 1) * WIDTH] for k in range(K)], axis=1)
        )
    mixed = jnp.dot(
        jnp.concatenate(pieces, axis=0), mix_ref[...], preferred_element_type=jnp.float32
    )
    out_ref[0] = mixed[:cols]


def disco_update(extended, base, mix, cols):
    rows = base.shape[0]
    width, channels = extended.shape[1:]

    def ext_spec(offset):
        return pl.BlockSpec((1, width, channels), lambda i: (i + offset, 0, 0))

    cell = pl.BlockSpec((1, cols, channels), lambda i: (i, 0, 0))
    return pl.pallas_call(
        disco_body,
        grid=(rows,),
        in_specs=[
            ext_spec(0),
            ext_spec(1),
            ext_spec(2),
            pl.BlockSpec((1, K, LANES), lambda i: (i, 0, 0)),
            pl.BlockSpec(mix.shape, lambda i: (0, 0)),
        ],
        out_specs=cell,
        out_shape=jax.ShapeDtypeStruct((rows, cols, channels), jnp.float32),
        scratch_shapes=[pltpu.VMEM((K * WIDTH, LANES), jnp.bfloat16)],
        compiler_params=pltpu.CompilerParams(vmem_limit_bytes=48 * 2**20),
        cost_estimate=pl.CostEstimate(
            flops=2 * rows * cols * K * channels * 512, bytes_accessed=12 * 2**20, transcendentals=0
        ),
        name="disco",
    )(extended, extended, extended, base, mix)


def norm_body(state_ref, gain_ref, out_ref):
    out_ref[...] = layer_norm(state_ref[...], gain_ref[...][None]).astype(jnp.bfloat16)


def norm_update(state, gain):
    cols, rows, channels = state.shape
    step = max(size for size in range(1, STEP + 1) if cols % size == 0)
    cell = pl.BlockSpec((step, rows, channels), lambda i: (i, 0, 0))
    return pl.pallas_call(
        norm_body,
        grid=(cols // step,),
        in_specs=[cell, pl.BlockSpec(gain.shape, lambda i: (0, 0))],
        out_specs=cell,
        out_shape=jax.ShapeDtypeStruct(state.shape, jnp.bfloat16),
        compiler_params=pltpu.CompilerParams(vmem_limit_bytes=48 * 2**20),
        name="norm",
    )(state, gain)


def mlp_body(state_ref, disco_ref, spectral_ref, gain_ref, in_ref, out_mat_ref, out_ref):
    cells = state_ref.shape[0] * state_ref.shape[1]
    channels = state_ref.shape[2]
    spectral = jnp.concatenate(
        [spectral_ref[n].astype(jnp.float32) for n in range(spectral_ref.shape[0])], axis=1
    )
    state = (state_ref[...] + disco_ref[...] + spectral).reshape(cells, channels)
    normed = layer_norm(state, gain_ref[...]).astype(jnp.bfloat16)
    hidden = jax.nn.gelu(jnp.dot(normed, in_ref[...], preferred_element_type=jnp.float32))
    state = state + jnp.dot(
        hidden.astype(jnp.bfloat16), out_mat_ref[...], preferred_element_type=jnp.float32
    )
    out_ref[...] = state.reshape(out_ref.shape)


def mlp_update(state, disco, spectral, gain, mat_in, mat_out):
    cols, rows, channels = state.shape
    lon_parts, share = spectral.shape[0], spectral.shape[2]
    step = max(size for size in range(1, STEP + 1) if cols % size == 0)
    cell = pl.BlockSpec((step, rows, channels), lambda i: (i, 0, 0))
    return pl.pallas_call(
        mlp_body,
        grid=(cols // step,),
        in_specs=[cell, cell]
        + [pl.BlockSpec((lon_parts, step, share, channels), lambda i: (0, i, 0, 0))]
        + [pl.BlockSpec(mat.shape, lambda i: (0, 0)) for mat in (gain, mat_in, mat_out)],
        out_specs=cell,
        out_shape=jax.ShapeDtypeStruct(state.shape, jnp.float32),
        compiler_params=pltpu.CompilerParams(vmem_limit_bytes=48 * 2**20),
        name="mlp",
    )(state, disco, spectral, gain, mat_in, mat_out)


def local(state, norm_gain, disco_kernel, taps, counts, disco_mix, filter_gain, mlp_in, mlp_out):
    lat_rows, lon_cols, channels = state.shape
    lon_parts = lax.axis_size("lon")
    lat_parts = lax.axis_size("lat")
    parts = lon_parts * lat_parts
    lon_total = lon_cols * lon_parts
    lat_total = lat_rows * lat_parts
    rank = lax.axis_index("lat") * lon_parts + lax.axis_index("lon")
    modes_own = M // parts
    tap_span = 2 * R + 1

    share = lat_rows // lon_parts
    turned = jnp.transpose(state, (1, 0, 2))
    normed = norm_update(turned, norm_gain[0, 0:1])

    slot_ids = jnp.arange(2 * M, dtype=jnp.int32)
    imaginary = slot_ids // modes_own % 2 == 1
    slot_modes = slot_ids // (2 * modes_own) * modes_own + slot_ids % modes_own
    points = jnp.arange(lon_total, dtype=jnp.int32)
    normed, slot_modes = lax.optimization_barrier((normed, slot_modes))
    sent = jnp.transpose(normed.reshape(lon_cols, lon_parts, share, channels), (1, 0, 2, 3))
    whole_rows = lax.all_to_all(sent, "lon", split_axis=0, concat_axis=0, tiled=True)
    whole_rows = whole_rows.reshape(lon_total, share, channels)
    normed = jnp.transpose(normed, (1, 0, 2))
    above, below = halo(normed, "lat", 0, 1, False)
    whole_rows, above, below = lax.optimization_barrier((whole_rows, above, below))
    quarter = jnp.where(imaginary, lon_total // 4, 0)
    steps = (slot_modes[:, None] * points[None, :] + quarter[:, None]) % lon_total
    waves = jnp.cos(steps.astype(jnp.float32) * (2.0 * math.pi / lon_total)).astype(jnp.bfloat16)
    waves = lax.optimization_barrier(waves)

    own_modes = rank * modes_own + jnp.arange(modes_own, dtype=jnp.int32)
    factor = jnp.where(own_modes == 0, 1.0, 2.0).astype(jnp.float32)
    legendre = legendre_table(own_modes, lat_total, L)
    weights = math.pi * jnp.sin(colatitudes(lat_total)) / (lat_total * lon_total)
    weighted = (legendre * (factor[:, None] * weights[None, :])[None]).astype(jnp.bfloat16)
    legendre = legendre.astype(jnp.bfloat16)

    live = jnp.arange(S, dtype=jnp.int32)[None, :] < counts[:, None]
    lanes = taps // tap_span * REACH + taps % tap_span
    matches = (lanes[:, :, None] == jnp.arange(LANES, dtype=jnp.int32)) & live[:, :, None]
    base = jnp.einsum(
        "isq,isk->ikq", matches.astype(jnp.float32), disco_kernel[0], precision=exact_prec
    )

    extended = jnp.concatenate([above, normed, below], axis=0)
    west, east = halo(extended, "lon", 1, R, True)
    blocks = -(-lon_cols // WIDTH)
    spare = blocks * WIDTH - lon_cols

    spectrum = jnp.einsum(
        "mp,pic->mic", waves, whole_rows, preferred_element_type=jnp.float32
    ).astype(jnp.bfloat16)
    owned = lax.all_to_all(spectrum, ("lat", "lon"), split_axis=0, concat_axis=0, tiled=True)
    owned, west, east = lax.optimization_barrier((owned, west, east))
    extended = jnp.concatenate(
        [west, extended, east, jnp.zeros((lat_rows + 2, spare, channels), jnp.bfloat16)], axis=1
    )
    disco = jnp.transpose(disco_update(extended, base, disco_mix[0], lon_cols), (1, 0, 2))
    owned = owned.reshape(parts, 2, modes_own, share, channels)
    owned = jnp.transpose(owned, (0, 3, 1, 2, 4)).reshape(lat_total, 2, modes_own, channels)
    coefficient = jnp.einsum(
        "lmj,jrmc->mlrc", weighted, owned, preferred_element_type=jnp.float32
    )
    scaled = (coefficient * filter_gain[0][None, :, None, :]).astype(jnp.bfloat16)
    filtered = jnp.einsum(
        "lmj,mlrc->mjrc", legendre, scaled, preferred_element_type=jnp.float32
    ).astype(jnp.bfloat16)
    filtered = jnp.transpose(filtered, (1, 2, 0, 3)).reshape(lat_total, 2 * modes_own, channels)
    returned = lax.all_to_all(filtered, ("lat", "lon"), split_axis=0, concat_axis=1, tiled=True)
    restored = jnp.einsum(
        "mp,imc->pic", waves, returned, preferred_element_type=jnp.float32
    ).astype(jnp.bfloat16)
    restored = restored.reshape(lon_parts, lon_cols, share, channels)
    spectral = lax.all_to_all(restored, "lon", split_axis=0, concat_axis=0, tiled=True)
    result = mlp_update(turned, disco, spectral, norm_gain[0, 1:2], mlp_in[0], mlp_out[0])
    return jnp.transpose(result, (1, 0, 2))


def solution(mesh):
    in_specs = (
        P(("grp", "lat"), "lon", None),
        P(),
        P(None, "lat", None, None),
        P("lat", None),
        P("lat"),
        P(),
        P(),
        P(),
        P(),
    )
    out_specs = P(("grp", "lat"), "lon", None)
    return jax.shard_map(local, mesh=mesh, in_specs=in_specs, out_specs=out_specs, check_vma=False)
```
